32 devices in a mesh: wide: 8 (over z, core), narrow: 4 (over y, x).
Axes of the slice: x: 2, y: 2, z: 4, core: 2. Of those that a mesh axis runs over, the one named last changes fastest.
Arguments:
- density: float32 [128, 2, 512, 512], P(('wide', 'narrow')), may hold values from -6 to 6
- hamiltonian: bfloat16 [2, 512, 512], replicated, may hold values from -0.1875 to 0.1875
- left_operators: bfloat16 [7, 2, 512, 512], replicated, may hold values from -0.25 to 0.25
- right_operators: bfloat16 [7, 2, 512, 512], replicated, may hold values from -0.25 to 0.25
- block_mask: int32 [7, 2, 8, 8], replicated, may hold values 0 or 1
- operator_slot: int32 [7], replicated, may hold values from 0 to 6, each once
- flip_sign: int32 [7], replicated, may hold values from 0 to 1
- damping_rate: float32 [7], replicated, may hold values from 0.2 to 2
- lower_weight: float32 [7], replicated, may hold values from 0.5 to 2
Outputs:
- derivative: float32 [128, 2, 512, 512], P(('wide', 'narrow'))
The draws below stay inside these ranges and needn't reach their ends.
Inputs may be any that keep to these rules, and one draw needn't show every extreme that they name: `operator_slot`: each of the 7 slots is used by exactly one mode.
All inputs are finite; a program needn't handle non-finite values.
Results may differ from the reference program's by a relative error of at most 0.0023.
Values may be sent and summed in bfloat16 or wider, within the bound.
No kernel may reach another device: no remote copies, remote signals or barrier semaphores. Data moves between devices by JAX's collectives and lax.ppermute only.
A program may use at most 256 MiB of HBM per device.

```python
import math
import jax
import jax.numpy as jnp
import numpy as np
from jax import lax

N = 512
BS = 64
MODES = 7
NB = 8
ADOS = 128


def with_ends(drawn, rng, smallest, largest):
    spot = [jax.random.randint(jax.random.fold_in(rng, axis), (), 0, length) for axis, length in enumerate(drawn.shape)]
    longest = drawn.shape.index(max(drawn.shape))
    next_to = spot[:longest] + [(spot[longest] + 1) % drawn.shape[longest]] + spot[longest + 1:]
    return drawn.at[tuple(spot)].set(smallest).at[tuple(next_to)].set(largest)


def shard_levels(own_key, shape, split, smallest, top_value):
    factor_of = 1.0
    for dim, shards_of in split:
        steps = jax.random.uniform(jax.random.fold_in(jax.random.fold_in(own_key, 6), dim), (shards_of,), jnp.float32, smallest / len(split), top_value / len(split))
        factor_of = factor_of * jnp.repeat(jnp.exp(steps), shape[dim] // shards_of).reshape((-1,) + (1,) * (len(shape) - 1 - dim))
    return factor_of


def noise(own_key, extent, width, most, shards=(), kind=jnp.bfloat16):
    values = width * jax.random.normal(own_key, extent, jnp.float32)
    if shards:
        values = values * shard_levels(own_key, extent, shards, -0.22, 0.18)
    return jnp.clip(values, -most, most).astype(kind)


def setup_inputs(seed: int = 0) -> dict:
    splits = jax.random.split(jax.random.key(seed), 10)
    return {
        "density": noise(splits[0], (ADOS, 2, N, N), 1.0, 6.0, ((0, 32),), jnp.float32),
        "hamiltonian": noise(splits[1], (2, N, N), (2 * N) ** -0.5, 0.1875),
        "left_operators": noise(splits[2], (MODES, 2, N, N), N ** -0.5, 0.25),
        "right_operators": noise(splits[3], (MODES, 2, N, N), N ** -0.5, 0.25),
        "block_mask": with_ends((jax.random.randint(splits[4], (MODES, 2, NB, NB), 0, 8) < 3).astype(jnp.int32), jax.random.fold_in(splits[4], 1), 0, 1),
        "operator_slot": jax.random.permutation(splits[5], MODES).astype(jnp.int32),
        "flip_sign": with_ends(jax.random.randint(splits[6], (MODES,), 0, 2), jax.random.fold_in(splits[6], 1), 0, 1).astype(jnp.int32),
        "damping_rate": jnp.clip(jnp.exp(jax.random.uniform(splits[7], (MODES,), jnp.float32, math.log(0.2), math.log(2.0))), 0.2, 2.0),
        "lower_weight": jnp.clip(jnp.exp(jax.random.uniform(splits[8], (MODES,), jnp.float32, math.log(0.5), math.log(2.0))), 0.5, 2.0),
    }


def left_product(operator, batch):
    first = operator.astype(jnp.float32)
    second = batch.astype(jnp.float32)
    high = lax.Precision.HIGHEST
    real = jnp.einsum("ij,ljk->lik", first[0], second[:, 0], precision=high) - jnp.einsum("ij,ljk->lik", first[1], second[:, 1], precision=high)
    imag = jnp.einsum("ij,ljk->lik", first[0], second[:, 1], precision=high) + jnp.einsum("ij,ljk->lik", first[1], second[:, 0], precision=high)
    return jnp.stack([real, imag], axis=1)


def right_product(batch, operator):
    first = batch.astype(jnp.float32)
    second = operator.astype(jnp.float32)
    high = lax.Precision.HIGHEST
    real = jnp.einsum("lij,jk->lik", first[:, 0], second[0], precision=high) - jnp.einsum("lij,jk->lik", first[:, 1], second[1], precision=high)
    imag = jnp.einsum("lij,jk->lik", first[:, 0], second[1], precision=high) + jnp.einsum("lij,jk->lik", first[:, 1], second[0], precision=high)
    return jnp.stack([real, imag], axis=1)


def reference(density, hamiltonian, left_operators, right_operators, block_mask, operator_slot, flip_sign, damping_rate, lower_weight):
    indices = np.arange(ADOS)
    bit_table = (indices[:, None] >> np.arange(MODES)[None, :]) & 1
    expanded = jnp.repeat(jnp.repeat(block_mask, BS, axis=2), BS, axis=3).astype(jnp.bfloat16)
    left_masked = left_operators * expanded[:, 0][:, None]
    right_masked = right_operators * expanded[:, 1][:, None]
    rounded = density.astype(jnp.bfloat16)
    commutator = left_product(hamiltonian, rounded) - right_product(rounded, hamiltonian)
    result = jnp.stack([commutator[:, 1], -commutator[:, 0]], axis=1)
    occupied = jnp.asarray(bit_table, dtype=jnp.float32)
    rates = jnp.sum(occupied * damping_rate[None, :], axis=1)
    result = result - rates[:, None, None, None] * density
    for flip_mode in range(MODES):
        partner = rounded[indices ^ (1 << flip_mode)]
        slot = operator_slot[flip_mode]
        term = left_product(left_masked[slot], partner) + right_product(partner, right_masked[slot])
        below = bit_table[:, :flip_mode].sum(axis=1) % 2
        parity = jnp.asarray(1 - 2 * below, dtype=jnp.float32)
        sign_value = (1 - 2 * flip_sign[flip_mode]).astype(jnp.float32)
        weight = jnp.where(occupied[:, flip_mode] > 0.5, lower_weight[flip_mode], jnp.float32(1.0))
        coef = parity * sign_value * weight
        result = result + coef[:, None, None, None] * term
    return result
```

```python
import functools

import jax
import jax.numpy as jnp
from jax import lax
from jax.experimental import pallas as pl
from jax.experimental.pallas import tpu as pltpu
from jax.sharding import PartitionSpec as P

VMEM_LIMIT = 56 * 2**20
COST = 1.0
SMEM = pl.BlockSpec(memory_space=pltpu.SMEM)


def params(flops, moved):
    return dict(
        compiler_params=pltpu.CompilerParams(
            vmem_limit_bytes=VMEM_LIMIT, dimension_semantics=("arbitrary",)
        ),
        cost_estimate=pl.CostEstimate(
            flops=int(COST * flops), bytes_accessed=int(COST * moved), transcendentals=0
        ),
    )


def dot(a, b):
    return jnp.dot(a, b, preferred_element_type=jnp.float32)


def round_kernel(groups, density_ref, _, *out_refs):
    step = pl.program_id(0)
    first_seen = min(first for first, _, _ in groups)
    for (first, span, part), out_ref in zip(groups, out_refs):

        @pl.when((step + first_seen >= first) & (step + first_seen < first + span))
        def _(part=part, out_ref=out_ref):
            if part is None:
                out_ref[...] = density_ref[...].astype(jnp.bfloat16)
            else:
                out_ref[0, 0] = density_ref[0, part].astype(jnp.bfloat16)


def round_groups(density, groups, after):
    n = density.shape[-1]
    low = min(first for first, _, _ in groups)
    high = max(first + span for first, span, _ in groups)

    def out_spec(first, span, part):
        return pl.BlockSpec(
            (1, 2 if part is None else 1, n, n),
            lambda g: (jnp.clip(g + low - first, 0, span - 1), 0, 0, 0),
        )

    return pl.pallas_call(
        functools.partial(round_kernel, groups),
        grid=(high - low,),
        in_specs=[
            pl.BlockSpec((1, 2, n, n), lambda g: (g + low, 0, 0, 0)),
            pl.BlockSpec(memory_space=pl.ANY),
        ],
        out_specs=[out_spec(*group) for group in groups],
        out_shape=[
            jax.ShapeDtypeStruct((span, 2 if part is None else 1, n, n), jnp.bfloat16)
            for _, span, part in groups
        ],
        **params(0, 8 * n * n * (high - low) + sum(4 * n * n * span for _, span, _ in groups)),
    )(density, after)


def operator_kernel(slot_ref, mask_ref, left_ref, right_ref, ham_ref, lout_ref, rout_ref):
    step = pl.program_id(0)
    last = pl.num_programs(0) - 1
    blocks = mask_ref.shape[2]
    n = left_ref.shape[2]
    size = n // blocks

    @pl.when(step < last)
    def _():
        lane = lax.broadcasted_iota(jnp.int32, (blocks, n), 1)
        row = lax.broadcasted_iota(jnp.int32, (blocks, n), 0)
        spread = jnp.where((lane >= row * size) & (lane < (row + 1) * size), 1.0, 0.0)
        for side, (src, dst) in enumerate(((left_ref, lout_ref), (right_ref, rout_ref))):
            wide = dot(mask_ref[0, side].astype(jnp.float32), spread).astype(jnp.bfloat16)
            for i in range(blocks):
                rows = slice(i * size, (i + 1) * size)
                for part in range(2):
                    dst[0, part, rows, :] = src[0, part, rows, :] * wide[i : i + 1, :]

    @pl.when(step == last)
    def _():
        lout_ref[0, 0] = ham_ref[1]
        lout_ref[0, 1] = -ham_ref[0]
        rout_ref[0, 0] = -ham_ref[1]
        rout_ref[0, 1] = ham_ref[0]


def make_operators(left_operators, right_operators, block_mask, operator_slot, hamiltonian):
    modes, _, n, _ = left_operators.shape
    block = (1, 2, n, n)

    def slot_of(g, slot):
        return (slot[jnp.minimum(g, modes - 1)], 0, 0, 0)

    operator = pl.BlockSpec(block, slot_of)
    out = pl.BlockSpec(block, lambda g, slot: (g, 0, 0, 0))
    shape = jax.ShapeDtypeStruct((modes + 1, 2, n, n), jnp.bfloat16)
    return pl.pallas_call(
        operator_kernel,
        grid_spec=pltpu.PrefetchScalarGridSpec(
            num_scalar_prefetch=1,
            grid=(modes + 1,),
            in_specs=[
                pl.BlockSpec((1,) + block_mask.shape[1:], slot_of),
                operator,
                operator,
                pl.BlockSpec((2, n, n), lambda g, slot: (0, 0, 0)),
            ],
            out_specs=[out, out],
        ),
        out_shape=[shape, shape],
        **params(0, 16 * (modes + 1) * n * n),
    )(operator_slot, block_mask, left_operators, right_operators, hamiltonian)


def term_kernel(first, terms, fresh, coef_ref, base_ref, *refs):
    out_ref = refs[-1]
    index = first + pl.program_id(0)
    if fresh:
        rate = -coef_ref[index, coef_ref.shape[1] - 1]
        real, imag = rate * base_ref[0, 0], rate * base_ref[0, 1]
    else:
        real, imag = base_ref[0, 0], base_ref[0, 1]
    for t, (mode, part) in enumerate(terms):
        rho, left, right = refs[3 * t : 3 * t + 3]
        coef = coef_ref[index, mode]
        lr, li, rr, ri = left[0, 0], left[0, 1], right[0, 0], right[0, 1]
        if part is None:
            a, b = rho[0, 0], rho[0, 1]
            real += coef * (dot(lr, a) - dot(li, b) + dot(a, rr) - dot(b, ri))
            imag += coef * (dot(lr, b) + dot(li, a) + dot(a, ri) + dot(b, rr))
        elif part == 0:
            a = rho[0, 0]
            real += coef * (dot(lr, a) + dot(a, rr))
            imag += coef * (dot(li, a) + dot(a, ri))
        else:
            b = rho[0, 0]
            real -= coef * (dot(li, b) + dot(b, ri))
            imag += coef * (dot(lr, b) + dot(b, rr))
    out_ref[0, 0] = real
    out_ref[0, 1] = imag


def add_terms(base, coef, operators, first, span, terms, fresh=False):
    n = base.shape[-1]
    lefts, rights = operators
    specs, args = [], []
    for mode, part, array, place in terms:
        specs.append(
            pl.BlockSpec((1, 2 if part is None else 1, n, n), lambda g, place=place: (place(g), 0, 0, 0))
        )
        operator = pl.BlockSpec((1, 2, n, n), lambda g, mode=mode: (mode, 0, 0, 0))
        specs += [operator, operator]
        args += [array, lefts, rights]
    block = pl.BlockSpec((1, 2, n, n), lambda g: (first + g, 0, 0, 0))
    return pl.pallas_call(
        functools.partial(term_kernel, first, [t[:2] for t in terms], fresh),
        grid=(span,),
        in_specs=[SMEM, block] + specs,
        out_specs=block,
        out_shape=jax.ShapeDtypeStruct(base.shape, jnp.float32),
        input_output_aliases={} if fresh else {1: 0},
        **params(
            16 * n**3 * span * sum(1 if t[1] is None else 0.5 for t in terms),
            n * n * span * (16 + 4 * len(terms)) + 8 * n * n * len(terms),
        ),
    )(coef, base, *args)


def flip(value, axis, bit):
    pairs = [(source, source ^ (1 << bit)) for source in range(lax.axis_size(axis))]
    return lax.ppermute(value, axis, pairs)


def coefficients(count, modes, flip_sign, damping_rate, lower_weight):
    first = (lax.axis_index("wide") * lax.axis_size("narrow") + lax.axis_index("narrow")) * count
    indices = first + jnp.arange(count, dtype=jnp.int32)
    bits = indices[:, None] >> jnp.arange(modes, dtype=jnp.int32)[None, :] & 1
    parity = 1 - 2 * ((jnp.cumsum(bits, axis=1) - bits) % 2)
    sign = parity * (1 - 2 * flip_sign)[None, :]
    coef = sign.astype(jnp.float32) * jnp.where(bits > 0, lower_weight[None, :], jnp.float32(1.0))
    rates = jnp.sum(bits.astype(jnp.float32) * damping_rate[None, :], axis=1)
    return jnp.concatenate([coef, jnp.ones((count, 1), jnp.float32), rates[:, None]], axis=1)


def body(
    density,
    hamiltonian,
    left_operators,
    right_operators,
    block_mask,
    operator_slot,
    flip_sign,
    damping_rate,
    lower_weight,
):
    count = density.shape[0]
    modes = left_operators.shape[0]
    local_bits = count.bit_length() - 1
    narrow_bits = lax.axis_size("narrow").bit_length() - 1
    last = count - 1

    def axis_of(mode):
        if mode < local_bits + narrow_bits:
            return "narrow", mode - local_bits
        return "wide", mode - local_bits - narrow_bits

    remote = list(range(local_bits, modes))
    slow = remote[-2:][::-1]
    near = [m for m in remote[:-2] if axis_of(m) == ("wide", 0)]
    middle = [m for m in remote[:-2] if m not in near]

    half = count // 2
    pieces = [(0, half), (half, last - half)] if half else [(0, last)]
    pieces = [(first, span, None) for first, span in pieces if span > 0]
    plan = [(near, 0, count, None)]
    plan += [([m], 0, last or count, None) for m in middle[:1]]
    for place, piece in enumerate(pieces):
        plan.append((slow,) + piece)
        if place == 0:
            plan += [([m], 0, count, None) for m in middle[1:]]
            middle = middle[:1]
    plan += [([m], last, 1, None) for m in middle[:1] if last]
    plan += [([m], 0, count, None) for m in middle[1:]]
    plan += [(slow, last, 1, 0), (slow, last, 1, 1)]
    plan = [step for step in plan if step[0]]

    groups = list(dict.fromkeys([(0, count, None)] + [step[1:] for step in plan]))
    early = [step[1:] for step in plan if step[0] == slow][:1]
    late = [group for group in groups if group not in early]
    rounded = dict(zip(early, round_groups(density, early, damping_rate)))
    rounded.update(zip(late, round_groups(density, late, rounded[early[0]])))

    sent = [[flip(rounded[step[1:]], *axis_of(m)) for m in step[0]] for step in plan]
    coef = coefficients(count, modes, flip_sign, damping_rate, lower_weight)
    operators = make_operators(
        left_operators, right_operators, block_mask, operator_slot, hamiltonian
    )
    whole = rounded[(0, count, None)]

    terms = [(modes, None, whole, lambda g: g)]
    for mode in range(local_bits):
        terms.append((mode, None, whole, lambda g, mode=mode: g ^ (1 << mode)))
    if near:
        terms += [(m, None, array, lambda g: g) for m, array in zip(near, sent[0])]
        plan, sent = plan[1:], sent[1:]
    result = add_terms(density, coef, operators, 0, count, terms, fresh=True)
    for (step_modes, first, span, part), arrays in zip(plan, sent):
        terms = [(m, part, array, lambda g: g) for m, array in zip(step_modes, arrays)]
        result = add_terms(result, coef, operators, first, span, terms)
    return result


def solution(mesh):
    placed = (P(("wide", "narrow"), None, None, None), P(), P(), P(), P(), P(), P(), P(), P())
    return jax.shard_map(
        body,
        mesh=mesh,
        in_specs=placed,
        out_specs=P(("wide", "narrow"), None, None, None),
        check_vma=False,
    )
```

```python
import functools

import jax
import jax.numpy as jnp
from jax import lax
from jax.experimental import pallas as pl
from jax.experimental.pallas import tpu as pltpu
from jax.sharding import PartitionSpec as P

VMEM_LIMIT = 56 * 2**20
LAST_VMEM_LIMIT = 24 * 2**20
SMEM = pl.BlockSpec(memory_space=pltpu.SMEM)


def params(flops, moved):
    return dict(
        compiler_params=pltpu.CompilerParams(
            vmem_limit_bytes=VMEM_LIMIT, dimension_semantics=("arbitrary",)
        ),
        cost_estimate=pl.CostEstimate(
            flops=flops, bytes_accessed=moved, transcendentals=0
        ),
    )


def dot(a, b):
    return jnp.dot(a, b, preferred_element_type=jnp.float32)


def round_kernel(groups, low, high, density_ref, _, *refs):
    outs, (source, loads, stores, *rounded) = refs[: len(groups)], refs[len(groups) :]
    pairs = [(index, part) for index in range(low, high) for part in range(2)]
    reads = {
        pair: pltpu.make_async_copy(density_ref.at[pair], source.at[place], loads.at[place])
        for place, pair in enumerate(pairs)
    }
    for pair in pairs:
        reads[pair].start()
    writes = []
    for place, (index, part) in enumerate(pairs):
        reads[index, part].wait()
        kept = rounded[0].at[place]
        kept[...] = source[place].astype(jnp.bfloat16)
        for (first, span, only), out_ref in zip(groups, outs):
            if first <= index < first + span and only in (None, part):
                target = out_ref.at[index - first, part if only is None else 0]
                writes.append(pltpu.make_async_copy(kept, target, stores.at[len(writes)]))
                writes[-1].start()
    for write in writes:
        write.wait()


def round_groups(density, groups, after):
    n = density.shape[-1]
    low = min(first for first, _, _ in groups)
    high = max(first + span for first, span, _ in groups)
    parts = 2 * (high - low)
    writes = sum(span * (2 if part is None else 1) for _, span, part in groups)
    anywhere = pl.BlockSpec(memory_space=pl.ANY)
    return pl.pallas_call(
        functools.partial(round_kernel, groups, low, high),
        in_specs=[anywhere, anywhere],
        out_specs=[anywhere] * len(groups),
        out_shape=[
            jax.ShapeDtypeStruct((span, 2 if part is None else 1, n, n), jnp.bfloat16)
            for _, span, part in groups
        ],
        scratch_shapes=[
            pltpu.VMEM((parts, n, n), jnp.float32),
            pltpu.SemaphoreType.DMA((parts,)),
            pltpu.SemaphoreType.DMA((writes,)),
            pltpu.VMEM((parts, n, n), jnp.bfloat16),
        ],
        compiler_params=pltpu.CompilerParams(vmem_limit_bytes=VMEM_LIMIT),
        cost_estimate=pl.CostEstimate(
            flops=0, bytes_accessed=n * n * (4 * parts + 2 * writes), transcendentals=0
        ),
    )(density, after)


def operator_kernel(slot_ref, mask_ref, left_ref, right_ref, ham_ref, lout_ref, rout_ref):
    step = pl.program_id(0)
    last = pl.num_programs(0) - 1
    blocks = mask_ref.shape[2]
    n = left_ref.shape[2]
    size = n // blocks

    @pl.when(step < last)
    def _():
        lane = lax.broadcasted_iota(jnp.int32, (blocks, n), 1)
        row = lax.broadcasted_iota(jnp.int32, (blocks, n), 0)
        spread = jnp.where((lane >= row * size) & (lane < (row + 1) * size), 1.0, 0.0)
        for side, (src, dst) in enumerate(((left_ref, lout_ref), (right_ref, rout_ref))):
            wide = dot(mask_ref[0, side].astype(jnp.float32), spread).astype(jnp.bfloat16)
            for i in range(blocks):
                rows = slice(i * size, (i + 1) * size)
                for part in range(2):
                    dst[0, part, rows, :] = src[0, part, rows, :] * wide[i : i + 1, :]

    @pl.when(step == last)
    def _():
        lout_ref[0, 0] = ham_ref[1]
        lout_ref[0, 1] = -ham_ref[0]
        rout_ref[0, 0] = -ham_ref[1]
        rout_ref[0, 1] = ham_ref[0]


def make_operators(left_operators, right_operators, block_mask, operator_slot, hamiltonian):
    modes, _, n, _ = left_operators.shape
    block = (1, 2, n, n)

    def slot_of(g, slot):
        return (slot[jnp.minimum(g, modes - 1)], 0, 0, 0)

    operator = pl.BlockSpec(block, slot_of)
    out = pl.BlockSpec(block, lambda g, slot: (g, 0, 0, 0))
    shape = jax.ShapeDtypeStruct((modes + 1, 2, n, n), jnp.bfloat16)
    return pl.pallas_call(
        operator_kernel,
        grid_spec=pltpu.PrefetchScalarGridSpec(
            num_scalar_prefetch=1,
            grid=(modes + 1,),
            in_specs=[
                pl.BlockSpec((1,) + block_mask.shape[1:], slot_of),
                operator,
                operator,
                pl.BlockSpec((2, n, n), lambda g, slot: (0, 0, 0)),
            ],
            out_specs=[out, out],
        ),
        out_shape=[shape, shape],
        **params(0, 16 * (modes + 1) * n * n),
    )(operator_slot, block_mask, left_operators, right_operators, hamiltonian)


def term_kernel(first, terms, fresh, coef_ref, base_ref, _, *refs):
    out_ref = refs[-1]
    index = first + pl.program_id(0)
    if fresh:
        rate = -coef_ref[index, coef_ref.shape[1] - 1]
        real, imag = rate * base_ref[0, 0], rate * base_ref[0, 1]
    else:
        real, imag = base_ref[0, 0], base_ref[0, 1]
    for t, (mode, part) in enumerate(terms):
        rho, left, right = refs[3 * t : 3 * t + 3]
        coef = coef_ref[index, mode]
        lr, li, rr, ri = left[0, 0], left[0, 1], right[0, 0], right[0, 1]
        if part is None:
            a, b = rho[0, 0], rho[0, 1]
            real += coef * (dot(lr, a) - dot(li, b) + dot(a, rr) - dot(b, ri))
            imag += coef * (dot(lr, b) + dot(li, a) + dot(a, ri) + dot(b, rr))
        elif part == 0:
            a = rho[0, 0]
            real += coef * (dot(lr, a) + dot(a, rr))
            imag += coef * (dot(li, a) + dot(a, ri))
        else:
            b = rho[0, 0]
            real -= coef * (dot(li, b) + dot(b, ri))
            imag += coef * (dot(lr, b) + dot(b, rr))
    out_ref[0, 0] = real
    out_ref[0, 1] = imag


def add_terms(base, into, coef, operators, first, span, terms):
    fresh = into is not base
    alias = {1: 0} if not fresh else {2: 0} if into is not None else {}
    into = into if fresh and into is not None else coef
    n = base.shape[-1]
    lefts, rights = operators
    specs, args = [], []
    for mode, part, array, place in terms:
        specs.append(
            pl.BlockSpec((1, 2 if part is None else 1, n, n), lambda g, place=place: (place(g), 0, 0, 0))
        )
        operator = pl.BlockSpec((1, 2, n, n), lambda g, mode=mode: (mode, 0, 0, 0))
        specs += [operator, operator]
        args += [array, lefts, rights]
    block = pl.BlockSpec((1, 2, n, n), lambda g: (first + g, 0, 0, 0))
    return pl.pallas_call(
        functools.partial(term_kernel, first, [t[:2] for t in terms], fresh),
        grid=(span,),
        in_specs=[SMEM, block, pl.BlockSpec(memory_space=pl.ANY)] + specs,
        out_specs=block,
        out_shape=jax.ShapeDtypeStruct(base.shape, jnp.float32),
        input_output_aliases=alias,
        **params(
            16 * n**3 * span * sum(1 if t[1] is None else 0.5 for t in terms),
            n * n * span * (16 + 4 * len(terms)) + 8 * n * n * len(terms),
        ),
    )(coef, base, into, *args)


def part_terms(index, out, terms, coef_ref, arrays, left, right):
    change = None
    for t, (mode, part) in enumerate(terms):
        use = part if out == 0 else 1 - part
        coef = coef_ref[index, mode]
        if out == 0 and part == 1:
            coef = -coef
        value = arrays[t][0, 0]
        term = coef * (dot(left[t, use], value) + dot(value, right[t, use]))
        change = term if change is None else change + term
    return change


def stage_kernel(index, terms, coef_ref, base_ref, left_ref, right_ref, *refs):
    count = len(terms)
    arrays, (total, left, right, loads) = refs[:count], refs[count:]
    copies = [pltpu.make_async_copy(base_ref.at[index], total, loads.at[0])]
    for t, (mode, _) in enumerate(terms):
        for source, target in ((left_ref, left), (right_ref, right)):
            copies.append(
                pltpu.make_async_copy(source.at[mode], target.at[t], loads.at[len(copies)])
            )
    for copy in copies:
        copy.start()
    for copy in copies:
        copy.wait()
    for out in range(2):
        total[out] += part_terms(index, out, terms, coef_ref, arrays, left, right)


def finish_kernel(index, terms, coef_ref, _, total, left, right, *refs):
    count = len(terms)
    arrays, (out_ref, result, stores) = refs[:count], refs[count:]
    writes = []
    for out in range(2):
        result[out] = total[out] + part_terms(index, out, terms, coef_ref, arrays, left, right)
        writes.append(
            pltpu.make_async_copy(result.at[out], out_ref.at[index, out], stores.at[out])
        )
        writes[-1].start()
    for write in writes:
        write.wait()


def in_vmem(array):
    return pltpu.with_memory_space_constraint(array, pltpu.VMEM)


def in_hbm(array):
    return pltpu.with_memory_space_constraint(array, pltpu.HBM)


def last_params(n, count):
    return dict(
        compiler_params=pltpu.CompilerParams(vmem_limit_bytes=LAST_VMEM_LIMIT),
        cost_estimate=pl.CostEstimate(
            flops=8 * n**3 * count, bytes_accessed=n * n * (8 + 8 * count), transcendentals=0
        ),
    )


ANYWHERE = pl.BlockSpec(memory_space=pl.ANY)
WHOLE = pl.BlockSpec(memory_space=pltpu.VMEM)


def stage_last(base, coef, operators, index, terms):
    n = base.shape[-1]
    count = len(terms)
    return pl.pallas_call(
        functools.partial(stage_kernel, index, [t[:2] for t in terms]),
        in_specs=[SMEM] + [ANYWHERE] * 3 + [WHOLE] * count,
        out_specs=[WHOLE] * 3,
        out_shape=[
            pltpu.VMEM((2, n, n), jnp.float32),
            pltpu.VMEM((count, 2, n, n), jnp.bfloat16),
            pltpu.VMEM((count, 2, n, n), jnp.bfloat16),
        ],
        scratch_shapes=[pltpu.SemaphoreType.DMA((1 + 2 * count,))],
        **last_params(n, count),
    )(coef, *[in_hbm(array) for array in (base, *operators)], *[in_vmem(t[2]) for t in terms])


def finish_last(base, coef, staged, index, terms):
    n = base.shape[-1]
    count = len(terms)
    return pl.pallas_call(
        functools.partial(finish_kernel, index, [t[:2] for t in terms]),
        in_specs=[SMEM, ANYWHERE] + [WHOLE] * (3 + count),
        out_specs=ANYWHERE,
        out_shape=jax.ShapeDtypeStruct(base.shape, jnp.float32),
        scratch_shapes=[pltpu.VMEM((2, n, n), jnp.float32), pltpu.SemaphoreType.DMA((2,))],
        input_output_aliases={1: 0},
        **last_params(n, count),
    )(coef, base, *[in_vmem(part) for part in staged], *[in_vmem(t[2]) for t in terms])


def flip(value, axis, bit):
    pairs = [(source, source ^ (1 << bit)) for source in range(lax.axis_size(axis))]
    return lax.ppermute(value, axis, pairs)


def coefficients(count, modes, flip_sign, damping_rate, lower_weight):
    first = (lax.axis_index("wide") * lax.axis_size("narrow") + lax.axis_index("narrow")) * count
    indices = first + jnp.arange(count, dtype=jnp.int32)
    bits = indices[:, None] >> jnp.arange(modes, dtype=jnp.int32)[None, :] & 1
    parity = 1 - 2 * ((jnp.cumsum(bits, axis=1) - bits) % 2)
    sign = parity * (1 - 2 * flip_sign)[None, :]
    coef = sign.astype(jnp.float32) * jnp.where(bits > 0, lower_weight[None, :], jnp.float32(1.0))
    rates = jnp.sum(bits.astype(jnp.float32) * damping_rate[None, :], axis=1)
    return jnp.concatenate([coef, jnp.ones((count, 1), jnp.float32), rates[:, None]], axis=1)


def body(
    density,
    hamiltonian,
    left_operators,
    right_operators,
    block_mask,
    operator_slot,
    flip_sign,
    damping_rate,
    lower_weight,
):
    count = density.shape[0]
    modes = left_operators.shape[0]
    local_bits = count.bit_length() - 1
    narrow_bits = lax.axis_size("narrow").bit_length() - 1
    last = count - 1

    def axis_of(mode):
        if mode < local_bits + narrow_bits:
            return "narrow", mode - local_bits
        return "wide", mode - local_bits - narrow_bits

    remote = list(range(local_bits, modes))
    slow = remote[-2:][::-1]
    near = [m for m in remote[:-2] if axis_of(m) == ("wide", 0)]
    middle = [m for m in remote[:-2] if m not in near]

    half = count // 2
    spans = [(0, half), (half, half)] if half else [(0, count)]
    pieces = [piece for piece in ((0, half), (half, last - half)) if piece[1]]
    plan = [(near,) + span + (None,) for span in spans]
    plan.append((middle[:1], 0, last or count, None))
    plan += [(slow,) + piece + (None,) for piece in pieces[:1]]
    plan.append((middle[1:], 0, count, None))
    plan += [(slow,) + piece + (None,) for piece in pieces[1:]]
    if last:
        plan.append((middle[:1], last, 1, None))
    plan += [(slow, last, 1, part) for part in range(2)]

    plan = [step for place, step in enumerate(plan) if step[0] or place < len(spans)]

    groups = list(dict.fromkeys([step[1:] for step in plan]))
    early = [step[1:] for step in plan if step[0] is slow][:1]
    late = [group for group in groups if group not in early]
    rounded = dict(zip(early, round_groups(density, early, damping_rate)))
    rounded.update(zip(late, round_groups(density, late, rounded[early[0]])))

    sent = [[flip(rounded[step[1:]], *axis_of(m)) for m in step[0]] for step in plan]
    coef = coefficients(count, modes, flip_sign, damping_rate, lower_weight)
    operators = make_operators(
        left_operators, right_operators, block_mask, operator_slot, hamiltonian
    )

    def local_terms(span):
        own, other = rounded[span + (None,)], rounded[(half - span[0],) + span[1:] + (None,)]
        terms = [(modes, None, own, lambda g: g)]
        for mode in range(local_bits):
            step = 1 << mode
            if step < span[1]:
                terms.append((mode, None, own, lambda g, step=step: g ^ step))
            else:
                terms.append((mode, None, other, lambda g: g))
        return terms

    result, staged = None, None
    for place, ((step_modes, first, span, part), arrays) in enumerate(zip(plan, sent)):
        terms = [(m, part, array, lambda g: g) for m, array in zip(step_modes, arrays)]
        if place < len(spans):
            terms = local_terms(spans[place]) + terms
            result = add_terms(density, result, coef, operators, first, span, terms)
        elif part is None:
            result = add_terms(result, result, coef, operators, first, span, terms)
        elif part == 0:
            staged = stage_last(result, coef, operators, first, terms)
        else:
            result = finish_last(result, coef, staged, first, terms)
    return result


def solution(mesh):
    placed = (P(("wide", "narrow"), None, None, None), P(), P(), P(), P(), P(), P(), P(), P())
    return jax.shard_map(
        body,
        mesh=mesh,
        in_specs=placed,
        out_specs=P(("wide", "narrow"), None, None, None),
        check_vma=False,
    )
```

```python
import functools

import jax
import jax.numpy as jnp
from jax import lax
from jax.experimental import pallas as pl
from jax.experimental.pallas import tpu as pltpu
from jax.sharding import PartitionSpec as P

VMEM_LIMIT = 56 * 2**20
LAST_VMEM_LIMIT = 24 * 2**20
SMEM = pl.BlockSpec(memory_space=pltpu.SMEM)


def params(flops, moved):
    return dict(
        compiler_params=pltpu.CompilerParams(
            vmem_limit_bytes=VMEM_LIMIT, dimension_semantics=("arbitrary",)
        ),
        cost_estimate=pl.CostEstimate(
            flops=flops, bytes_accessed=moved, transcendentals=0
        ),
    )


def dot(a, b):
    return jnp.dot(a, b, preferred_element_type=jnp.float32)


def round_kernel(groups, low, high, density_ref, _, *refs):
    outs, (source, loads, stores, *rounded) = refs[: len(groups)], refs[len(groups) :]
    pairs = [(index, part) for index in range(low, high) for part in range(2)]
    reads = {
        pair: pltpu.make_async_copy(density_ref.at[pair], source.at[place], loads.at[place])
        for place, pair in enumerate(pairs)
    }
    for pair in pairs:
        reads[pair].start()
    writes = []
    for place, (index, part) in enumerate(pairs):
        reads[index, part].wait()
        kept = rounded[0].at[place]
        kept[...] = source[place].astype(jnp.bfloat16)
        for (first, span, cut), out_ref in zip(groups, outs):
            if not first <= index < first + span or cut and cut[0] != part:
                continue
            rows = pl.ds(cut[1], cut[2]) if cut else pl.ds(0, kept.shape[0])
            target = out_ref.at[index - first, 0 if cut else part]
            writes.append(pltpu.make_async_copy(kept.at[rows], target, stores.at[len(writes)]))
            writes[-1].start()
    for write in writes:
        write.wait()


def round_first_kernel(low, density_ref, out_ref, source, loads):
    span, parts = out_ref.shape[:2]
    pairs = [(index, part) for index in range(span) for part in range(parts)]
    reads = [
        pltpu.make_async_copy(
            density_ref.at[low + index, part], source.at[index, part], loads.at[place]
        )
        for place, (index, part) in enumerate(pairs)
    ]
    for read in reads:
        read.start()
    for read, pair in zip(reads, pairs):
        read.wait()
        out_ref[pair] = source[pair].astype(jnp.bfloat16)


def round_first(density, group):
    n = density.shape[-1]
    low, span, _ = group
    return pl.pallas_call(
        functools.partial(round_first_kernel, low),
        in_specs=[pl.BlockSpec(memory_space=pl.ANY)],
        out_specs=pl.BlockSpec(memory_space=pltpu.VMEM),
        out_shape=pltpu.VMEM((span, 2, n, n), jnp.bfloat16),
        scratch_shapes=[
            pltpu.VMEM((span, 2, n, n), jnp.float32),
            pltpu.SemaphoreType.DMA((2 * span,)),
        ],
        compiler_params=pltpu.CompilerParams(vmem_limit_bytes=VMEM_LIMIT),
        cost_estimate=pl.CostEstimate(
            flops=0, bytes_accessed=n * n * 12 * span, transcendentals=0
        ),
    )(density)


def round_groups(density, groups, after):
    n = density.shape[-1]
    low = min(first for first, _, _ in groups)
    high = max(first + span for first, span, _ in groups)
    parts = 2 * (high - low)
    shapes = [(span, 1, cut[2], n) if cut else (span, 2, n, n) for _, span, cut in groups]
    writes = sum(shape[0] * shape[1] for shape in shapes)
    anywhere = pl.BlockSpec(memory_space=pl.ANY)
    return pl.pallas_call(
        functools.partial(round_kernel, groups, low, high),
        in_specs=[anywhere, anywhere],
        out_specs=[anywhere] * len(groups),
        out_shape=[jax.ShapeDtypeStruct(shape, jnp.bfloat16) for shape in shapes],
        scratch_shapes=[
            pltpu.VMEM((parts, n, n), jnp.float32),
            pltpu.SemaphoreType.DMA((parts,)),
            pltpu.SemaphoreType.DMA((writes,)),
            pltpu.VMEM((parts, n, n), jnp.bfloat16),
        ],
        compiler_params=pltpu.CompilerParams(vmem_limit_bytes=VMEM_LIMIT),
        cost_estimate=pl.CostEstimate(
            flops=0, bytes_accessed=n * n * (4 * parts + 2 * writes), transcendentals=0
        ),
    )(density, after)


def operator_kernel(slot_ref, mask_ref, left_ref, right_ref, ham_ref, lout_ref, rout_ref):
    step = pl.program_id(0)
    last = pl.num_programs(0) - 1
    blocks = mask_ref.shape[2]
    n = left_ref.shape[2]
    size = n // blocks

    @pl.when(step < last)
    def _():
        lane = lax.broadcasted_iota(jnp.int32, (blocks, n), 1)
        row = lax.broadcasted_iota(jnp.int32, (blocks, n), 0)
        spread = jnp.where((lane >= row * size) & (lane < (row + 1) * size), 1.0, 0.0)
        for side, (src, dst) in enumerate(((left_ref, lout_ref), (right_ref, rout_ref))):
            wide = dot(mask_ref[0, side].astype(jnp.float32), spread).astype(jnp.bfloat16)
            for i in range(blocks):
                rows = slice(i * size, (i + 1) * size)
                for part in range(2):
                    dst[0, part, rows, :] = src[0, part, rows, :] * wide[i : i + 1, :]

    @pl.when(step == last)
    def _():
        lout_ref[0, 0] = ham_ref[1]
        lout_ref[0, 1] = -ham_ref[0]
        rout_ref[0, 0] = -ham_ref[1]
        rout_ref[0, 1] = ham_ref[0]


def make_operators(left_operators, right_operators, block_mask, operator_slot, hamiltonian):
    modes, _, n, _ = left_operators.shape
    block = (1, 2, n, n)

    def slot_of(g, slot):
        return (slot[jnp.minimum(g, modes - 1)], 0, 0, 0)

    operator = pl.BlockSpec(block, slot_of)
    out = pl.BlockSpec(block, lambda g, slot: (g, 0, 0, 0))
    shape = jax.ShapeDtypeStruct((modes + 1, 2, n, n), jnp.bfloat16)
    return pl.pallas_call(
        operator_kernel,
        grid_spec=pltpu.PrefetchScalarGridSpec(
            num_scalar_prefetch=1,
            grid=(modes + 1,),
            in_specs=[
                pl.BlockSpec((1,) + block_mask.shape[1:], slot_of),
                operator,
                operator,
                pl.BlockSpec((2, n, n), lambda g, slot: (0, 0, 0)),
            ],
            out_specs=[out, out],
        ),
        out_shape=[shape, shape],
        **params(0, 16 * (modes + 1) * n * n),
    )(operator_slot, block_mask, left_operators, right_operators, hamiltonian)


def term_kernel(first, terms, fresh, coef_ref, base_ref, _, *refs):
    out_ref = refs[-1]
    index = first + pl.program_id(0)
    if fresh:
        rate = -coef_ref[index, coef_ref.shape[1] - 1]
        real, imag = rate * base_ref[0, 0], rate * base_ref[0, 1]
    else:
        real, imag = base_ref[0, 0], base_ref[0, 1]
    for t, mode in enumerate(terms):
        rho, left, right = refs[3 * t : 3 * t + 3]
        coef = coef_ref[index, mode]
        lr, li, rr, ri = left[0, 0], left[0, 1], right[0, 0], right[0, 1]
        a, b = rho[0, 0], rho[0, 1]
        real += coef * (dot(lr, a) - dot(li, b) + dot(a, rr) - dot(b, ri))
        imag += coef * (dot(lr, b) + dot(li, a) + dot(a, ri) + dot(b, rr))
    out_ref[0, 0] = real
    out_ref[0, 1] = imag


def add_terms(base, into, coef, operators, first, span, terms):
    fresh = into is not base
    alias = {1: 0} if not fresh else {2: 0} if into is not None else {}
    into = into if fresh and into is not None else coef
    n = base.shape[-1]
    lefts, rights = operators
    specs, args = [], []
    for mode, array, place in terms:
        specs.append(pl.BlockSpec((1, 2, n, n), lambda g, place=place: (place(g), 0, 0, 0)))
        operator = pl.BlockSpec((1, 2, n, n), lambda g, mode=mode: (mode, 0, 0, 0))
        specs += [operator, operator]
        args += [array, lefts, rights]
    block = pl.BlockSpec((1, 2, n, n), lambda g: (first + g, 0, 0, 0))
    return pl.pallas_call(
        functools.partial(term_kernel, first, [t[0] for t in terms], fresh),
        grid=(span,),
        in_specs=[SMEM, block, pl.BlockSpec(memory_space=pl.ANY)] + specs,
        out_specs=block,
        out_shape=jax.ShapeDtypeStruct(base.shape, jnp.float32),
        input_output_aliases=alias,
        **params(
            16 * n**3 * span * len(terms),
            n * n * span * (16 + 4 * len(terms)) + 8 * n * n * len(terms),
        ),
    )(coef, base, into, *args)


def add_piece(index, modes, cut, out, rows, coef_ref, arrays, left, right, sum_in, sum_out):
    part, first, size = cut
    use = part if out == 0 else 1 - part
    own = max(first, rows[0]), min(first + size, rows[1])
    total = sum_in[out, rows[0] : rows[1]]
    for t, mode in enumerate(modes):
        coef = coef_ref[index, mode]
        coef = -coef if out == 0 and part == 1 else coef
        total += coef * dot(left[t, use, rows[0] : rows[1], first : first + size], arrays[t][0, 0])
    sum_out[out, rows[0] : rows[1]] = total
    if own[0] < own[1]:
        total = sum_out[out, own[0] : own[1]]
        for t, mode in enumerate(modes):
            coef = coef_ref[index, mode]
            coef = -coef if out == 0 and part == 1 else coef
            value = arrays[t][0, 0, own[0] - first : own[1] - first]
            total += coef * dot(value, right[t, use])
        sum_out[out, own[0] : own[1]] = total


def first_piece_kernel(index, modes, cut, coef_ref, base_ref, left_ref, right_ref, *refs):
    count = len(modes)
    arrays, (total, left, right, loads) = refs[:count], refs[count:]
    copies = [pltpu.make_async_copy(base_ref.at[index], total, loads.at[0])]
    for t, mode in enumerate(modes):
        for source, target in ((left_ref, left), (right_ref, right)):
            copies.append(
                pltpu.make_async_copy(source.at[mode], target.at[t], loads.at[len(copies)])
            )
    for copy in copies:
        copy.start()
    for copy in copies:
        copy.wait()
    rows = 0, total.shape[1]
    for out in range(2):
        add_piece(index, modes, cut, out, rows, coef_ref, arrays, left, right, total, total)


def next_piece_kernel(index, modes, cut, coef_ref, total, left, right, *refs):
    arrays, out_ref = refs[:-1], refs[-1]
    rows = 0, total.shape[1]
    for out in range(2):
        add_piece(index, modes, cut, out, rows, coef_ref, arrays, left, right, total, out_ref)


def last_piece_kernel(index, modes, cut, coef_ref, _, total, left, right, *refs):
    count = len(modes)
    arrays, (out_ref, result, stores) = refs[:count], refs[count:]
    n = total.shape[1]
    bands = [(cut[1], cut[1] + cut[2]), (0, cut[1]), (cut[1] + cut[2], n)]
    writes = []
    for out in range(2):
        for rows in bands:
            if rows[0] == rows[1]:
                continue
            add_piece(index, modes, cut, out, rows, coef_ref, arrays, left, right, total, result)
            band = pl.ds(rows[0], rows[1] - rows[0])
            writes.append(
                pltpu.make_async_copy(
                    result.at[out, band], out_ref.at[index, out, band], stores.at[len(writes)]
                )
            )
            writes[-1].start()
    for write in writes:
        write.wait()


def in_vmem(array):
    return pltpu.with_memory_space_constraint(array, pltpu.VMEM)


def in_hbm(array):
    return pltpu.with_memory_space_constraint(array, pltpu.HBM)


ANYWHERE = pl.BlockSpec(memory_space=pl.ANY)
WHOLE = pl.BlockSpec(memory_space=pltpu.VMEM)


def piece_call(kernel, index, modes, cut, n, operands, arrays, out_shape, scratch, alias):
    moved = n * n * (16 + 8 * len(modes))
    out_specs = jax.tree.map(
        lambda shape: ANYWHERE if isinstance(shape, jax.ShapeDtypeStruct) else WHOLE, out_shape
    )
    return pl.pallas_call(
        functools.partial(kernel, index, modes, cut),
        in_specs=[SMEM] + [spec for _, spec in operands[1:]] + [WHOLE] * len(arrays),
        out_specs=out_specs,
        out_shape=out_shape,
        scratch_shapes=scratch,
        input_output_aliases=alias,
        compiler_params=pltpu.CompilerParams(vmem_limit_bytes=LAST_VMEM_LIMIT),
        cost_estimate=pl.CostEstimate(
            flops=8 * n * n * cut[2] * len(modes), bytes_accessed=moved, transcendentals=0
        ),
    )(*[array for array, _ in operands], *[in_vmem(array) for array in arrays])


def first_piece(base, coef, operators, index, modes, cut, arrays):
    n, count = base.shape[-1], len(modes)
    operands = [(coef, SMEM)] + [(in_hbm(array), ANYWHERE) for array in (base, *operators)]
    out_shape = [
        pltpu.VMEM((2, n, n), jnp.float32),
        pltpu.VMEM((count, 2, n, n), jnp.bfloat16),
        pltpu.VMEM((count, 2, n, n), jnp.bfloat16),
    ]
    scratch = [pltpu.SemaphoreType.DMA((1 + 2 * count,))]
    return piece_call(
        first_piece_kernel, index, modes, cut, n, operands, arrays, out_shape, scratch, {}
    )


def next_piece(staged, coef, index, modes, cut, arrays):
    n = staged[0].shape[-1]
    operands = [(coef, SMEM)] + [(in_vmem(array), WHOLE) for array in staged]
    out_shape = pltpu.VMEM((2, n, n), jnp.float32)
    total = piece_call(
        next_piece_kernel, index, modes, cut, n, operands, arrays, out_shape, [], {1: 0}
    )
    return [total] + list(staged[1:])


def last_piece(base, staged, coef, index, modes, cut, arrays):
    n = base.shape[-1]
    operands = [(coef, SMEM), (base, ANYWHERE)] + [(in_vmem(array), WHOLE) for array in staged]
    out_shape = jax.ShapeDtypeStruct(base.shape, jnp.float32)
    scratch = [pltpu.VMEM((2, n, n), jnp.float32), pltpu.SemaphoreType.DMA((6,))]
    return piece_call(
        last_piece_kernel, index, modes, cut, n, operands, arrays, out_shape, scratch, {1: 0}
    )


def flip(value, axis, bit):
    pairs = [(source, source ^ (1 << bit)) for source in range(lax.axis_size(axis))]
    return lax.ppermute(value, axis, pairs)


def coefficients(count, modes, flip_sign, damping_rate, lower_weight):
    first = (lax.axis_index("wide") * lax.axis_size("narrow") + lax.axis_index("narrow")) * count
    indices = first + jnp.arange(count, dtype=jnp.int32)
    bits = indices[:, None] >> jnp.arange(modes, dtype=jnp.int32)[None, :] & 1
    parity = 1 - 2 * ((jnp.cumsum(bits, axis=1) - bits) % 2)
    sign = parity * (1 - 2 * flip_sign)[None, :]
    coef = sign.astype(jnp.float32) * jnp.where(bits > 0, lower_weight[None, :], jnp.float32(1.0))
    rates = jnp.sum(bits.astype(jnp.float32) * damping_rate[None, :], axis=1)
    return jnp.concatenate([coef, jnp.ones((count, 1), jnp.float32), rates[:, None]], axis=1)


def body(
    density,
    hamiltonian,
    left_operators,
    right_operators,
    block_mask,
    operator_slot,
    flip_sign,
    damping_rate,
    lower_weight,
):
    count = density.shape[0]
    modes = left_operators.shape[0]
    local_bits = count.bit_length() - 1
    narrow_bits = lax.axis_size("narrow").bit_length() - 1
    last = count - 1

    def axis_of(mode):
        if mode < local_bits + narrow_bits:
            return "narrow", mode - local_bits
        return "wide", mode - local_bits - narrow_bits

    remote = list(range(local_bits, modes))
    slow = remote[-2:][::-1]
    near = [m for m in remote[:-2] if axis_of(m) == ("wide", 0)]
    middle = [m for m in remote[:-2] if m not in near]

    half = count // 2
    spans = [(0, half), (half, half)] if half else [(0, count)]
    pieces = [piece for piece in ((0, half), (half, last - half)) if piece[1]]
    plan = [(near,) + span + (None,) for span in spans]
    plan.append((middle[:1], 0, last or count, None))
    plan += [(slow,) + piece + (None,) for piece in pieces[:1]]
    plan.append((middle[1:], 0, count, None))
    plan += [(slow,) + piece + (None,) for piece in pieces[1:]]
    if last:
        plan.append((middle[:1], last, 1, None))
    n = density.shape[-1]
    cuts = [(0, 0, n), (1, 0, n // 2), (1, n // 2, n // 2)]
    plan += [(slow, last, 1, cut) for cut in cuts]

    plan = [step for place, step in enumerate(plan) if step[0] or place < len(spans)]

    groups = list(dict.fromkeys([step[1:] for step in plan]))
    early = [step[1:] for step in plan if step[0] is slow][:1]
    late = [group for group in groups if group not in early]
    if early[0][2] is None:
        rounded = {early[0]: round_first(density, early[0])}
    else:
        rounded = dict(zip(early, round_groups(density, early, damping_rate)))
    rounded.update(zip(late, round_groups(density, late, rounded[early[0]])))

    sent = [[flip(rounded[step[1:]], *axis_of(m)) for m in step[0]] for step in plan]
    coef = coefficients(count, modes, flip_sign, damping_rate, lower_weight)
    operators = make_operators(
        left_operators, right_operators, block_mask, operator_slot, hamiltonian
    )

    def local_terms(span):
        own, other = rounded[span + (None,)], rounded[(half - span[0],) + span[1:] + (None,)]
        terms = [(modes, own, lambda g: g)]
        for mode in range(local_bits):
            step = 1 << mode
            if step < span[1]:
                terms.append((mode, own, lambda g, step=step: g ^ step))
            else:
                terms.append((mode, other, lambda g: g))
        return terms

    result, staged = None, None
    for place, ((step_modes, first, span, cut), arrays) in enumerate(zip(plan, sent)):
        terms = [(m, array, lambda g: g) for m, array in zip(step_modes, arrays)]
        if place < len(spans):
            terms = local_terms(spans[place]) + terms
            result = add_terms(density, result, coef, operators, first, span, terms)
        elif cut is None:
            result = add_terms(result, result, coef, operators, first, span, terms)
        elif cut == cuts[0]:
            staged = first_piece(result, coef, operators, first, step_modes, cut, arrays)
        elif cut != cuts[-1]:
            staged = next_piece(staged, coef, first, step_modes, cut, arrays)
        else:
            result = last_piece(result, staged, coef, first, step_modes, cut, arrays)
    return result


def solution(mesh):
    placed = (P(("wide", "narrow"), None, None, None), P(), P(), P(), P(), P(), P(), P(), P())
    return jax.shard_map(
        body,
        mesh=mesh,
        in_specs=placed,
        out_specs=P(("wide", "narrow"), None, None, None),
        check_vma=False,
    )
```

```python
import functools

import jax
import jax.numpy as jnp
from jax import lax
from jax.experimental import pallas as pl
from jax.experimental.pallas import tpu as pltpu
from jax.sharding import PartitionSpec as P

VMEM_LIMIT = 56 * 2**20
LAST_VMEM_LIMIT = 24 * 2**20
SMEM = pl.BlockSpec(memory_space=pltpu.SMEM)


def params(flops, moved):
    return dict(
        compiler_params=pltpu.CompilerParams(
            vmem_limit_bytes=VMEM_LIMIT, dimension_semantics=("arbitrary",)
        ),
        cost_estimate=pl.CostEstimate(
            flops=flops, bytes_accessed=moved, transcendentals=0
        ),
    )


def dot(a, b):
    return jnp.dot(a, b, preferred_element_type=jnp.float32)


def round_kernel(groups, low, high, density_ref, _, *refs):
    outs, (source, loads, stores, *rounded) = refs[: len(groups)], refs[len(groups) :]
    pairs = [(index, part) for index in range(low, high) for part in range(2)]
    reads = {
        pair: pltpu.make_async_copy(density_ref.at[pair], source.at[place], loads.at[place])
        for place, pair in enumerate(pairs)
    }
    for pair in pairs:
        reads[pair].start()
    writes = []
    for place, (index, part) in enumerate(pairs):
        reads[index, part].wait()
        kept = rounded[0].at[place]
        kept[...] = source[place].astype(jnp.bfloat16)
        for (first, span, cut), out_ref in zip(groups, outs):
            if not first <= index < first + span or cut and cut[0] != part:
                continue
            rows = pl.ds(cut[1], cut[2]) if cut else pl.ds(0, kept.shape[0])
            target = out_ref.at[index - first, 0 if cut else part]
            writes.append(pltpu.make_async_copy(kept.at[rows], target, stores.at[len(writes)]))
            writes[-1].start()
    for write in writes:
        write.wait()


def round_first_kernel(low, density_ref, out_ref, source, loads):
    span, parts = out_ref.shape[:2]
    pairs = [(index, part) for index in range(span) for part in range(parts)]
    reads = [
        pltpu.make_async_copy(
            density_ref.at[low + index, part], source.at[index, part], loads.at[place]
        )
        for place, (index, part) in enumerate(pairs)
    ]
    for read in reads:
        read.start()
    for read, pair in zip(reads, pairs):
        read.wait()
        out_ref[pair] = source[pair].astype(jnp.bfloat16)


def round_first(density, group):
    n = density.shape[-1]
    low, span, _ = group
    return pl.pallas_call(
        functools.partial(round_first_kernel, low),
        in_specs=[pl.BlockSpec(memory_space=pl.ANY)],
        out_specs=pl.BlockSpec(memory_space=pltpu.VMEM),
        out_shape=pltpu.VMEM((span, 2, n, n), jnp.bfloat16),
        scratch_shapes=[
            pltpu.VMEM((span, 2, n, n), jnp.float32),
            pltpu.SemaphoreType.DMA((2 * span,)),
        ],
        compiler_params=pltpu.CompilerParams(vmem_limit_bytes=VMEM_LIMIT),
        cost_estimate=pl.CostEstimate(
            flops=0, bytes_accessed=n * n * 12 * span, transcendentals=0
        ),
    )(density)


def round_groups(density, groups, after):
    n = density.shape[-1]
    low = min(first for first, _, _ in groups)
    high = max(first + span for first, span, _ in groups)
    parts = 2 * (high - low)
    shapes = [(span, 1, cut[2], n) if cut else (span, 2, n, n) for _, span, cut in groups]
    writes = sum(shape[0] * shape[1] for shape in shapes)
    anywhere = pl.BlockSpec(memory_space=pl.ANY)
    return pl.pallas_call(
        functools.partial(round_kernel, groups, low, high),
        in_specs=[anywhere, anywhere],
        out_specs=[anywhere] * len(groups),
        out_shape=[jax.ShapeDtypeStruct(shape, jnp.bfloat16) for shape in shapes],
        scratch_shapes=[
            pltpu.VMEM((parts, n, n), jnp.float32),
            pltpu.SemaphoreType.DMA((parts,)),
            pltpu.SemaphoreType.DMA((writes,)),
            pltpu.VMEM((parts, n, n), jnp.bfloat16),
        ],
        compiler_params=pltpu.CompilerParams(vmem_limit_bytes=VMEM_LIMIT),
        cost_estimate=pl.CostEstimate(
            flops=0, bytes_accessed=n * n * (4 * parts + 2 * writes), transcendentals=0
        ),
    )(density, after)


def operator_kernel(slot_ref, mask_ref, left_ref, right_ref, ham_ref, lout_ref, rout_ref):
    step = pl.program_id(0)
    last = pl.num_programs(0) - 1
    blocks = mask_ref.shape[2]
    n = left_ref.shape[2]
    size = n // blocks

    @pl.when(step < last)
    def _():
        lane = lax.broadcasted_iota(jnp.int32, (blocks, n), 1)
        row = lax.broadcasted_iota(jnp.int32, (blocks, n), 0)
        spread = jnp.where((lane >= row * size) & (lane < (row + 1) * size), 1.0, 0.0)
        for side, (src, dst) in enumerate(((left_ref, lout_ref), (right_ref, rout_ref))):
            wide = dot(mask_ref[0, side].astype(jnp.float32), spread).astype(jnp.bfloat16)
            for i in range(blocks):
                rows = slice(i * size, (i + 1) * size)
                for part in range(2):
                    dst[0, part, rows, :] = src[0, part, rows, :] * wide[i : i + 1, :]

    @pl.when(step == last)
    def _():
        lout_ref[0, 0] = ham_ref[1]
        lout_ref[0, 1] = -ham_ref[0]
        rout_ref[0, 0] = -ham_ref[1]
        rout_ref[0, 1] = ham_ref[0]


def make_operators(left_operators, right_operators, block_mask, operator_slot, hamiltonian):
    modes, _, n, _ = left_operators.shape
    block = (1, 2, n, n)

    def slot_of(g, slot):
        return (slot[jnp.minimum(g, modes - 1)], 0, 0, 0)

    operator = pl.BlockSpec(block, slot_of)
    out = pl.BlockSpec(block, lambda g, slot: (g, 0, 0, 0))
    shape = jax.ShapeDtypeStruct((modes + 1, 2, n, n), jnp.bfloat16)
    return pl.pallas_call(
        operator_kernel,
        grid_spec=pltpu.PrefetchScalarGridSpec(
            num_scalar_prefetch=1,
            grid=(modes + 1,),
            in_specs=[
                pl.BlockSpec((1,) + block_mask.shape[1:], slot_of),
                operator,
                operator,
                pl.BlockSpec((2, n, n), lambda g, slot: (0, 0, 0)),
            ],
            out_specs=[out, out],
        ),
        out_shape=[shape, shape],
        **params(0, 16 * (modes + 1) * n * n),
    )(operator_slot, block_mask, left_operators, right_operators, hamiltonian)


def term_kernel(first, terms, fresh, coef_ref, base_ref, _, *refs):
    out_ref = refs[-1]
    index = first + pl.program_id(0)
    if fresh:
        rate = -coef_ref[index, coef_ref.shape[1] - 1]
        real, imag = rate * base_ref[0, 0], rate * base_ref[0, 1]
    else:
        real, imag = base_ref[0, 0], base_ref[0, 1]
    for t, mode in enumerate(terms):
        rho, left, right = refs[3 * t : 3 * t + 3]
        coef = coef_ref[index, mode]
        lr, li, rr, ri = left[0, 0], left[0, 1], right[0, 0], right[0, 1]
        a, b = rho[0, 0], rho[0, 1]
        real += coef * (dot(lr, a) - dot(li, b) + dot(a, rr) - dot(b, ri))
        imag += coef * (dot(lr, b) + dot(li, a) + dot(a, ri) + dot(b, rr))
    out_ref[0, 0] = real
    out_ref[0, 1] = imag


def add_terms(base, into, coef, operators, first, span, terms):
    fresh = into is not base
    alias = {1: 0} if not fresh else {2: 0} if into is not None else {}
    into = into if fresh and into is not None else coef
    n = base.shape[-1]
    lefts, rights = operators
    specs, args = [], []
    for mode, array, place in terms:
        specs.append(pl.BlockSpec((1, 2, n, n), lambda g, place=place: (place(g), 0, 0, 0)))
        operator = pl.BlockSpec((1, 2, n, n), lambda g, mode=mode: (mode, 0, 0, 0))
        specs += [operator, operator]
        args += [array, lefts, rights]
    block = pl.BlockSpec((1, 2, n, n), lambda g: (first + g, 0, 0, 0))
    return pl.pallas_call(
        functools.partial(term_kernel, first, [t[0] for t in terms], fresh),
        grid=(span,),
        in_specs=[SMEM, block, pl.BlockSpec(memory_space=pl.ANY)] + specs,
        out_specs=block,
        out_shape=jax.ShapeDtypeStruct(base.shape, jnp.float32),
        input_output_aliases=alias,
        **params(
            16 * n**3 * span * len(terms),
            n * n * span * (16 + 4 * len(terms)) + 8 * n * n * len(terms),
        ),
    )(coef, base, into, *args)


def bands_of(cut, n):
    _, first, size = cut
    bands = [(first, first + size), (0, first), (first + size, n)]
    return [rows for rows in bands if rows[0] < rows[1]]


def add_piece(modes, cut, out, rows, coefs, arrays, left, right, sum_in, sum_out):
    part, first, size = cut
    use = part if out == 0 else 1 - part
    total = sum_in[out, rows[0] : rows[1]]
    for t in range(len(modes)):
        coef = -coefs[t] if out == 0 and part == 1 else coefs[t]
        value = arrays[t][0, 0]
        change = dot(left[t, use, rows[0] : rows[1], first : first + size], value)
        if rows[0] == first:
            change += dot(value, right[t, use])
        total += coef * change
    sum_out[out, rows[0] : rows[1]] = total


def first_piece_kernel(index, modes, cut, coef_ref, base_ref, left_ref, right_ref, *refs):
    count = len(modes)
    arrays, (total, left, right, scale, loads) = refs[:count], refs[count:]
    copies = [pltpu.make_async_copy(base_ref.at[index], total, loads.at[0])]
    for t, mode in enumerate(modes):
        for source, target in ((left_ref, left), (right_ref, right)):
            copies.append(
                pltpu.make_async_copy(source.at[mode], target.at[t], loads.at[len(copies)])
            )
    for copy in copies:
        copy.start()
    coefs = [coef_ref[index, mode] for mode in modes]
    for t in range(count):
        scale[t] = jnp.full(scale.shape[1:], coefs[t])
    for copy in copies:
        copy.wait()
    for out in range(2):
        for rows in bands_of(cut, total.shape[1]):
            add_piece(modes, cut, out, rows, coefs, arrays, left, right, total, total)


def next_piece_kernel(index, modes, cut, total, left, right, scale, *refs):
    arrays, out_ref = refs[:-1], refs[-1]
    coefs = [scale[t, 0:1] for t in range(len(modes))]
    for out in range(2):
        for rows in bands_of(cut, total.shape[1]):
            add_piece(modes, cut, out, rows, coefs, arrays, left, right, total, out_ref)


def last_piece_kernel(index, modes, cut, _, total, left, right, scale, *refs):
    count = len(modes)
    arrays, (out_ref, result, stores) = refs[:count], refs[count:]
    coefs = [scale[t, 0:1] for t in range(count)]
    writes = []
    for out in range(2):
        for rows in bands_of(cut, total.shape[1]):
            add_piece(modes, cut, out, rows, coefs, arrays, left, right, total, result)
            band = pl.ds(rows[0], rows[1] - rows[0])
            writes.append(
                pltpu.make_async_copy(
                    result.at[out, band], out_ref.at[index, out, band], stores.at[len(writes)]
                )
            )
            writes[-1].start()
    for write in writes:
        write.wait()


def in_vmem(array):
    return pltpu.with_memory_space_constraint(array, pltpu.VMEM)


def in_hbm(array):
    return pltpu.with_memory_space_constraint(array, pltpu.HBM)


ANYWHERE = pl.BlockSpec(memory_space=pl.ANY)
WHOLE = pl.BlockSpec(memory_space=pltpu.VMEM)


def piece_call(kernel, index, modes, cut, n, operands, arrays, out_shape, scratch, alias):
    moved = n * n * (16 + 8 * len(modes))
    out_specs = jax.tree.map(
        lambda shape: ANYWHERE if isinstance(shape, jax.ShapeDtypeStruct) else WHOLE, out_shape
    )
    return pl.pallas_call(
        functools.partial(kernel, index, modes, cut),
        in_specs=[spec for _, spec in operands] + [WHOLE] * len(arrays),
        out_specs=out_specs,
        out_shape=out_shape,
        scratch_shapes=scratch,
        input_output_aliases=alias,
        compiler_params=pltpu.CompilerParams(vmem_limit_bytes=LAST_VMEM_LIMIT),
        cost_estimate=pl.CostEstimate(
            flops=8 * n * n * cut[2] * len(modes), bytes_accessed=moved, transcendentals=0
        ),
    )(*[array for array, _ in operands], *[in_vmem(array) for array in arrays])


def first_piece(base, coef, operators, index, modes, cut, arrays):
    n, count = base.shape[-1], len(modes)
    operands = [(coef, SMEM)] + [(in_hbm(array), ANYWHERE) for array in (base, *operators)]
    out_shape = [
        pltpu.VMEM((2, n, n), jnp.float32),
        pltpu.VMEM((count, 2, n, n), jnp.bfloat16),
        pltpu.VMEM((count, 2, n, n), jnp.bfloat16),
        pltpu.VMEM((count, 8, n), jnp.float32),
    ]
    scratch = [pltpu.SemaphoreType.DMA((1 + 2 * count,))]
    return piece_call(
        first_piece_kernel, index, modes, cut, n, operands, arrays, out_shape, scratch, {}
    )


def next_piece(staged, index, modes, cut, arrays):
    n = staged[0].shape[-1]
    operands = [(in_vmem(array), WHOLE) for array in staged]
    out_shape = pltpu.VMEM((2, n, n), jnp.float32)
    total = piece_call(
        next_piece_kernel, index, modes, cut, n, operands, arrays, out_shape, [], {0: 0}
    )
    return [total] + list(staged[1:])


def last_piece(base, staged, index, modes, cut, arrays):
    n = base.shape[-1]
    operands = [(base, ANYWHERE)] + [(in_vmem(array), WHOLE) for array in staged]
    out_shape = jax.ShapeDtypeStruct(base.shape, jnp.float32)
    scratch = [pltpu.VMEM((2, n, n), jnp.float32), pltpu.SemaphoreType.DMA((6,))]
    return piece_call(
        last_piece_kernel, index, modes, cut, n, operands, arrays, out_shape, scratch, {0: 0}
    )


def flip(value, axis, bit):
    pairs = [(source, source ^ (1 << bit)) for source in range(lax.axis_size(axis))]
    return lax.ppermute(value, axis, pairs)


def coefficients(count, modes, flip_sign, damping_rate, lower_weight):
    first = (lax.axis_index("wide") * lax.axis_size("narrow") + lax.axis_index("narrow")) * count
    indices = first + jnp.arange(count, dtype=jnp.int32)
    bits = indices[:, None] >> jnp.arange(modes, dtype=jnp.int32)[None, :] & 1
    parity = 1 - 2 * ((jnp.cumsum(bits, axis=1) - bits) % 2)
    sign = parity * (1 - 2 * flip_sign)[None, :]
    coef = sign.astype(jnp.float32) * jnp.where(bits > 0, lower_weight[None, :], jnp.float32(1.0))
    rates = jnp.sum(bits.astype(jnp.float32) * damping_rate[None, :], axis=1)
    return jnp.concatenate([coef, jnp.ones((count, 1), jnp.float32), rates[:, None]], axis=1)


def body(
    density,
    hamiltonian,
    left_operators,
    right_operators,
    block_mask,
    operator_slot,
    flip_sign,
    damping_rate,
    lower_weight,
):
    count = density.shape[0]
    modes = left_operators.shape[0]
    local_bits = count.bit_length() - 1
    narrow_bits = lax.axis_size("narrow").bit_length() - 1
    last = count - 1

    def axis_of(mode):
        if mode < local_bits + narrow_bits:
            return "narrow", mode - local_bits
        return "wide", mode - local_bits - narrow_bits

    remote = list(range(local_bits, modes))
    slow = remote[-2:][::-1]
    near = [m for m in remote[:-2] if axis_of(m) == ("wide", 0)]
    middle = [m for m in remote[:-2] if m not in near]

    half = count // 2
    spans = [(0, half), (half, half)] if half else [(0, count)]
    pieces = [piece for piece in ((0, half), (half, last - half)) if piece[1]]
    plan = [(near,) + span + (None,) for span in spans]
    plan.append((middle[:1], 0, last or count, None))
    plan += [(slow,) + piece + (None,) for piece in pieces[:1]]
    plan.append((middle[1:], 0, count, None))
    plan += [(slow,) + piece + (None,) for piece in pieces[1:]]
    if last:
        plan.append((middle[:1], last, 1, None))
    n = density.shape[-1]
    cuts = [(0, 0, n), (1, 0, n // 2), (1, n // 2, n // 2)]
    plan += [(slow, last, 1, cut) for cut in cuts]

    plan = [step for place, step in enumerate(plan) if step[0] or place < len(spans)]

    groups = list(dict.fromkeys([step[1:] for step in plan]))
    early = [step[1:] for step in plan if step[0] is slow][:1]
    late = [group for group in groups if group not in early]
    if early[0][2] is None:
        rounded = {early[0]: round_first(density, early[0])}
    else:
        rounded = dict(zip(early, round_groups(density, early, damping_rate)))
    rounded.update(zip(late, round_groups(density, late, rounded[early[0]])))

    sent = [[flip(rounded[step[1:]], *axis_of(m)) for m in step[0]] for step in plan]
    coef = coefficients(count, modes, flip_sign, damping_rate, lower_weight)
    operators = make_operators(
        left_operators, right_operators, block_mask, operator_slot, hamiltonian
    )

    def local_terms(span):
        own, other = rounded[span + (None,)], rounded[(half - span[0],) + span[1:] + (None,)]
        terms = [(modes, own, lambda g: g)]
        for mode in range(local_bits):
            step = 1 << mode
            if step < span[1]:
                terms.append((mode, own, lambda g, step=step: g ^ step))
            else:
                terms.append((mode, other, lambda g: g))
        return terms

    result, staged = None, None
    for place, ((step_modes, first, span, cut), arrays) in enumerate(zip(plan, sent)):
        terms = [(m, array, lambda g: g) for m, array in zip(step_modes, arrays)]
        if place < len(spans):
            terms = local_terms(spans[place]) + terms
            result = add_terms(density, result, coef, operators, first, span, terms)
        elif cut is None:
            result = add_terms(result, result, coef, operators, first, span, terms)
        elif cut == cuts[0]:
            staged = first_piece(result, coef, operators, first, step_modes, cut, arrays)
        elif cut != cuts[-1]:
            staged = next_piece(staged, first, step_modes, cut, arrays)
        else:
            result = last_piece(result, staged, first, step_modes, cut, arrays)
    return result


def solution(mesh):
    placed = (P(("wide", "narrow"), None, None, None), P(), P(), P(), P(), P(), P(), P(), P())
    return jax.shard_map(
        body,
        mesh=mesh,
        in_specs=placed,
        out_specs=P(("wide", "narrow"), None, None, None),
        check_vma=False,
    )
```

```python
import functools

import jax
import jax.numpy as jnp
from jax import lax
from jax.experimental import pallas as pl
from jax.experimental.pallas import tpu as pltpu
from jax.sharding import PartitionSpec as P

VMEM_LIMIT = 56 * 2**20
LAST_VMEM_LIMIT = 24 * 2**20
SMEM = pl.BlockSpec(memory_space=pltpu.SMEM)


def params(flops, moved):
    return dict(
        compiler_params=pltpu.CompilerParams(
            vmem_limit_bytes=VMEM_LIMIT, dimension_semantics=("arbitrary",)
        ),
        cost_estimate=pl.CostEstimate(
            flops=flops, bytes_accessed=moved, transcendentals=0
        ),
    )


def dot(a, b):
    return jnp.dot(a, b, preferred_element_type=jnp.float32)


def round_kernel(groups, low, high, density_ref, _, *refs):
    outs, (source, loads, stores, *rounded) = refs[: len(groups)], refs[len(groups) :]
    pairs = [(index, part) for index in range(low, high) for part in range(2)]
    reads = {
        pair: pltpu.make_async_copy(density_ref.at[pair], source.at[place], loads.at[place])
        for place, pair in enumerate(pairs)
    }
    for pair in pairs:
        reads[pair].start()
    writes = []
    for place, (index, part) in enumerate(pairs):
        reads[index, part].wait()
        kept = rounded[0].at[place]
        kept[...] = source[place].astype(jnp.bfloat16)
        for (first, span, cut), out_ref in zip(groups, outs):
            if not first <= index < first + span or cut and cut[0] != part:
                continue
            rows = pl.ds(cut[1], cut[2]) if cut else pl.ds(0, kept.shape[0])
            target = out_ref.at[index - first, 0 if cut else part]
            writes.append(pltpu.make_async_copy(kept.at[rows], target, stores.at[len(writes)]))
            writes[-1].start()
    for write in writes:
        write.wait()


def round_first_kernel(low, density_ref, out_ref, source, loads):
    span, parts = out_ref.shape[:2]
    pairs = [(index, part) for index in range(span) for part in range(parts)]
    reads = [
        pltpu.make_async_copy(
            density_ref.at[low + index, part], source.at[index, part], loads.at[place]
        )
        for place, (index, part) in enumerate(pairs)
    ]
    for read in reads:
        read.start()
    for read, pair in zip(reads, pairs):
        read.wait()
        out_ref[pair] = source[pair].astype(jnp.bfloat16)


def round_first(density, group):
    n = density.shape[-1]
    low, span, _ = group
    return pl.pallas_call(
        functools.partial(round_first_kernel, low),
        in_specs=[pl.BlockSpec(memory_space=pl.ANY)],
        out_specs=pl.BlockSpec(memory_space=pltpu.VMEM),
        out_shape=pltpu.VMEM((span, 2, n, n), jnp.bfloat16),
        scratch_shapes=[
            pltpu.VMEM((span, 2, n, n), jnp.float32),
            pltpu.SemaphoreType.DMA((2 * span,)),
        ],
        compiler_params=pltpu.CompilerParams(vmem_limit_bytes=VMEM_LIMIT),
        cost_estimate=pl.CostEstimate(
            flops=0, bytes_accessed=n * n * 12 * span, transcendentals=0
        ),
    )(density)


def round_groups(density, groups, after):
    n = density.shape[-1]
    low = min(first for first, _, _ in groups)
    high = max(first + span for first, span, _ in groups)
    parts = 2 * (high - low)
    shapes = [(span, 1, cut[2], n) if cut else (span, 2, n, n) for _, span, cut in groups]
    writes = sum(shape[0] * shape[1] for shape in shapes)
    anywhere = pl.BlockSpec(memory_space=pl.ANY)
    return pl.pallas_call(
        functools.partial(round_kernel, groups, low, high),
        in_specs=[anywhere, anywhere],
        out_specs=[anywhere] * len(groups),
        out_shape=[jax.ShapeDtypeStruct(shape, jnp.bfloat16) for shape in shapes],
        scratch_shapes=[
            pltpu.VMEM((parts, n, n), jnp.float32),
            pltpu.SemaphoreType.DMA((parts,)),
            pltpu.SemaphoreType.DMA((writes,)),
            pltpu.VMEM((parts, n, n), jnp.bfloat16),
        ],
        compiler_params=pltpu.CompilerParams(vmem_limit_bytes=VMEM_LIMIT),
        cost_estimate=pl.CostEstimate(
            flops=0, bytes_accessed=n * n * (4 * parts + 2 * writes), transcendentals=0
        ),
    )(density, after)


def operator_kernel(slot_ref, mask_ref, left_ref, right_ref, ham_ref, lout_ref, rout_ref):
    step = pl.program_id(0)
    last = pl.num_programs(0) - 1
    blocks = mask_ref.shape[2]
    n = left_ref.shape[2]
    size = n // blocks

    @pl.when(step < last)
    def _():
        lane = lax.broadcasted_iota(jnp.int32, (blocks, n), 1)
        row = lax.broadcasted_iota(jnp.int32, (blocks, n), 0)
        spread = jnp.where((lane >= row * size) & (lane < (row + 1) * size), 1.0, 0.0)
        for side, (src, dst) in enumerate(((left_ref, lout_ref), (right_ref, rout_ref))):
            wide = dot(mask_ref[0, side].astype(jnp.float32), spread).astype(jnp.bfloat16)
            for i in range(blocks):
                rows = slice(i * size, (i + 1) * size)
                for part in range(2):
                    dst[0, part, rows, :] = src[0, part, rows, :] * wide[i : i + 1, :]

    @pl.when(step == last)
    def _():
        lout_ref[0, 0] = ham_ref[1]
        lout_ref[0, 1] = -ham_ref[0]
        rout_ref[0, 0] = -ham_ref[1]
        rout_ref[0, 1] = ham_ref[0]


def make_operators(left_operators, right_operators, block_mask, operator_slot, hamiltonian):
    modes, _, n, _ = left_operators.shape
    block = (1, 2, n, n)

    def slot_of(g, slot):
        return (slot[jnp.minimum(g, modes - 1)], 0, 0, 0)

    operator = pl.BlockSpec(block, slot_of)
    out = pl.BlockSpec(block, lambda g, slot: (g, 0, 0, 0))
    shape = jax.ShapeDtypeStruct((modes + 1, 2, n, n), jnp.bfloat16)
    return pl.pallas_call(
        operator_kernel,
        grid_spec=pltpu.PrefetchScalarGridSpec(
            num_scalar_prefetch=1,
            grid=(modes + 1,),
            in_specs=[
                pl.BlockSpec((1,) + block_mask.shape[1:], slot_of),
                operator,
                operator,
                pl.BlockSpec((2, n, n), lambda g, slot: (0, 0, 0)),
            ],
            out_specs=[out, out],
        ),
        out_shape=[shape, shape],
        **params(0, 16 * (modes + 1) * n * n),
    )(operator_slot, block_mask, left_operators, right_operators, hamiltonian)


def term_kernel(first, terms, fresh, coef_ref, base_ref, _, *refs):
    out_ref = refs[-1]
    index = first + pl.program_id(0)
    if fresh:
        rate = -coef_ref[index, coef_ref.shape[1] - 1]
        real, imag = rate * base_ref[0, 0], rate * base_ref[0, 1]
    else:
        real, imag = base_ref[0, 0], base_ref[0, 1]
    for t, mode in enumerate(terms):
        rho, left, right = refs[3 * t : 3 * t + 3]
        coef = coef_ref[index, mode]
        lr, li, rr, ri = left[0, 0], left[0, 1], right[0, 0], right[0, 1]
        a, b = rho[0, 0], rho[0, 1]
        real += coef * (dot(lr, a) - dot(li, b) + dot(a, rr) - dot(b, ri))
        imag += coef * (dot(lr, b) + dot(li, a) + dot(a, ri) + dot(b, rr))
    out_ref[0, 0] = real
    out_ref[0, 1] = imag


def add_terms(base, into, coef, operators, first, span, terms):
    fresh = into is not base
    alias = {1: 0} if not fresh else {2: 0} if into is not None else {}
    into = into if fresh and into is not None else coef
    n = base.shape[-1]
    lefts, rights = operators
    specs, args = [], []
    for mode, array, place in terms:
        specs.append(pl.BlockSpec((1, 2, n, n), lambda g, place=place: (place(g), 0, 0, 0)))
        operator = pl.BlockSpec((1, 2, n, n), lambda g, mode=mode: (mode, 0, 0, 0))
        specs += [operator, operator]
        args += [array, lefts, rights]
    block = pl.BlockSpec((1, 2, n, n), lambda g: (first + g, 0, 0, 0))
    return pl.pallas_call(
        functools.partial(term_kernel, first, [t[0] for t in terms], fresh),
        grid=(span,),
        in_specs=[SMEM, block, pl.BlockSpec(memory_space=pl.ANY)] + specs,
        out_specs=block,
        out_shape=jax.ShapeDtypeStruct(base.shape, jnp.float32),
        input_output_aliases=alias,
        **params(
            16 * n**3 * span * len(terms),
            n * n * span * (16 + 4 * len(terms)) + 8 * n * n * len(terms),
        ),
    )(coef, base, into, *args)


def bands_of(cut, n):
    _, first, size = cut
    bands = [(first, first + size), (0, first), (first + size, n)]
    return [rows for rows in bands if rows[0] < rows[1]]


def add_piece(modes, cut, out, rows, coefs, arrays, left, right, sum_in, sum_out):
    part, first, size = cut
    use = part if out == 0 else 1 - part
    total = sum_in[out, rows[0] : rows[1]]
    for t in range(len(modes)):
        coef = -coefs[t] if out == 0 and part == 1 else coefs[t]
        value = arrays[t][0, 0]
        change = dot(left[t, use, rows[0] : rows[1], first : first + size], value)
        if rows[0] == first:
            change += dot(value, right[t, use])
        total += coef * change
    sum_out[out, rows[0] : rows[1]] = total


def first_piece_kernel(index, modes, cut, coef_ref, base_ref, left_ref, right_ref, *refs):
    count = len(modes)
    arrays, (total, left, right, scale, loads) = refs[:count], refs[count:]
    copies = [pltpu.make_async_copy(base_ref.at[index], total, loads.at[0])]
    for t, mode in enumerate(modes):
        for source, target in ((left_ref, left), (right_ref, right)):
            copies.append(
                pltpu.make_async_copy(source.at[mode], target.at[t], loads.at[len(copies)])
            )
    for copy in copies:
        copy.start()
    coefs = [coef_ref[index, mode] for mode in modes]
    for t in range(count):
        scale[t] = jnp.full(scale.shape[1:], coefs[t])
    for copy in copies:
        copy.wait()
    for out in range(2):
        for rows in bands_of(cut, total.shape[1]):
            add_piece(modes, cut, out, rows, coefs, arrays, left, right, total, total)


def next_piece_kernel(index, modes, cut, total, left, right, scale, *refs):
    arrays, out_ref = refs[:-1], refs[-1]
    coefs = [scale[t, 0:1] for t in range(len(modes))]
    for out in range(2):
        for rows in bands_of(cut, total.shape[1]):
            add_piece(modes, cut, out, rows, coefs, arrays, left, right, total, out_ref)


def last_piece_kernel(index, modes, cut, _, total, left, right, scale, *refs):
    count = len(modes)
    arrays, (out_ref, result, stores) = refs[:count], refs[count:]
    coefs = [scale[t, 0:1] for t in range(count)]
    writes = []
    for out in range(2):
        for rows in bands_of(cut, total.shape[1]):
            add_piece(modes, cut, out, rows, coefs, arrays, left, right, total, result)
            band = pl.ds(rows[0], rows[1] - rows[0])
            writes.append(
                pltpu.make_async_copy(
                    result.at[out, band], out_ref.at[index, out, band], stores.at[len(writes)]
                )
            )
            writes[-1].start()
    for write in writes:
        write.wait()


def in_vmem(array):
    return pltpu.with_memory_space_constraint(array, pltpu.VMEM)


def in_hbm(array):
    return pltpu.with_memory_space_constraint(array, pltpu.HBM)


ANYWHERE = pl.BlockSpec(memory_space=pl.ANY)
WHOLE = pl.BlockSpec(memory_space=pltpu.VMEM)


def piece_call(kernel, index, modes, cut, n, operands, arrays, out_shape, scratch, alias):
    moved = n * n * (16 + 8 * len(modes))
    out_specs = jax.tree.map(
        lambda shape: ANYWHERE if isinstance(shape, jax.ShapeDtypeStruct) else WHOLE, out_shape
    )
    return pl.pallas_call(
        functools.partial(kernel, index, modes, cut),
        in_specs=[spec for _, spec in operands] + [WHOLE] * len(arrays),
        out_specs=out_specs,
        out_shape=out_shape,
        scratch_shapes=scratch,
        input_output_aliases=alias,
        compiler_params=pltpu.CompilerParams(vmem_limit_bytes=LAST_VMEM_LIMIT),
        cost_estimate=pl.CostEstimate(
            flops=8 * n * n * cut[2] * len(modes), bytes_accessed=moved, transcendentals=0
        ),
    )(*[array for array, _ in operands], *[in_vmem(array) for array in arrays])


def first_piece(base, coef, operators, index, modes, cut, arrays):
    n, count = base.shape[-1], len(modes)
    operands = [(coef, SMEM)] + [(in_hbm(array), ANYWHERE) for array in (base, *operators)]
    out_shape = [
        pltpu.VMEM((2, n, n), jnp.float32),
        pltpu.VMEM((count, 2, n, n), jnp.bfloat16),
        pltpu.VMEM((count, 2, n, n), jnp.bfloat16),
        pltpu.VMEM((count, 8, n), jnp.float32),
    ]
    scratch = [pltpu.SemaphoreType.DMA((1 + 2 * count,))]
    return piece_call(
        first_piece_kernel, index, modes, cut, n, operands, arrays, out_shape, scratch, {}
    )


def next_piece(staged, index, modes, cut, arrays):
    n = staged[0].shape[-1]
    operands = [(in_vmem(array), WHOLE) for array in staged]
    out_shape = pltpu.VMEM((2, n, n), jnp.float32)
    total = piece_call(
        next_piece_kernel, index, modes, cut, n, operands, arrays, out_shape, [], {0: 0}
    )
    return [total] + list(staged[1:])


def last_piece(base, staged, index, modes, cut, arrays):
    n = base.shape[-1]
    operands = [(base, ANYWHERE)] + [(in_vmem(array), WHOLE) for array in staged]
    out_shape = jax.ShapeDtypeStruct(base.shape, jnp.float32)
    scratch = [pltpu.VMEM((2, n, n), jnp.float32), pltpu.SemaphoreType.DMA((6,))]
    return piece_call(
        last_piece_kernel, index, modes, cut, n, operands, arrays, out_shape, scratch, {0: 0}
    )


def flip(value, axis, bit):
    pairs = [(source, source ^ (1 << bit)) for source in range(lax.axis_size(axis))]
    return lax.ppermute(value, axis, pairs)


def coefficients(count, modes, flip_sign, damping_rate, lower_weight):
    first = (lax.axis_index("wide") * lax.axis_size("narrow") + lax.axis_index("narrow")) * count
    indices = first + jnp.arange(count, dtype=jnp.int32)
    bits = indices[:, None] >> jnp.arange(modes, dtype=jnp.int32)[None, :] & 1
    parity = 1 - 2 * ((jnp.cumsum(bits, axis=1) - bits) % 2)
    sign = parity * (1 - 2 * flip_sign)[None, :]
    coef = sign.astype(jnp.float32) * jnp.where(bits > 0, lower_weight[None, :], jnp.float32(1.0))
    rates = jnp.sum(bits.astype(jnp.float32) * damping_rate[None, :], axis=1)
    return jnp.concatenate([coef, jnp.ones((count, 1), jnp.float32), rates[:, None]], axis=1)


def body(
    density,
    hamiltonian,
    left_operators,
    right_operators,
    block_mask,
    operator_slot,
    flip_sign,
    damping_rate,
    lower_weight,
):
    count = density.shape[0]
    modes = left_operators.shape[0]
    local_bits = count.bit_length() - 1
    narrow_bits = lax.axis_size("narrow").bit_length() - 1
    last = count - 1

    def axis_of(mode):
        if mode < local_bits + narrow_bits:
            return "narrow", mode - local_bits
        return "wide", mode - local_bits - narrow_bits

    remote = list(range(local_bits, modes))
    slow = remote[-2:][::-1]
    near = [m for m in remote[:-2] if axis_of(m) == ("wide", 0)]
    middle = [m for m in remote[:-2] if m not in near]

    half = count // 2
    spans = [(0, half), (half, half)] if half else [(0, count)]
    pieces = [piece for piece in ((0, half), (half, last - half)) if piece[1]]
    plan = [(near,) + span + (None,) for span in spans]
    plan.append((middle[:1], 0, last or count, None))
    plan += [(slow,) + piece + (None,) for piece in pieces[:1]]
    plan.append((middle[1:], 0, count, None))
    plan += [(slow,) + piece + (None,) for piece in pieces[1:]]
    if last:
        plan.append((middle[:1], last, 1, None))
    n = density.shape[-1]
    cuts = [(0, 0, n), (1, 0, 3 * n // 4), (1, 3 * n // 4, n // 4)]
    plan += [(slow, last, 1, cut) for cut in cuts]

    plan = [step for place, step in enumerate(plan) if step[0] or place < len(spans)]

    groups = list(dict.fromkeys([step[1:] for step in plan]))
    early = [step[1:] for step in plan if step[0] is slow][:1]
    late = [group for group in groups if group not in early]
    if early[0][2] is None:
        rounded = {early[0]: round_first(density, early[0])}
    else:
        rounded = dict(zip(early, round_groups(density, early, damping_rate)))
    rounded.update(zip(late, round_groups(density, late, rounded[early[0]])))

    sent = [[flip(rounded[step[1:]], *axis_of(m)) for m in step[0]] for step in plan]
    coef = coefficients(count, modes, flip_sign, damping_rate, lower_weight)
    operators = make_operators(
        left_operators, right_operators, block_mask, operator_slot, hamiltonian
    )

    def local_terms(span):
        own, other = rounded[span + (None,)], rounded[(half - span[0],) + span[1:] + (None,)]
        terms = [(modes, own, lambda g: g)]
        for mode in range(local_bits):
            step = 1 << mode
            if step < span[1]:
                terms.append((mode, own, lambda g, step=step: g ^ step))
            else:
                terms.append((mode, other, lambda g: g))
        return terms

    result, staged = None, None
    for place, ((step_modes, first, span, cut), arrays) in enumerate(zip(plan, sent)):
        terms = [(m, array, lambda g: g) for m, array in zip(step_modes, arrays)]
        if place < len(spans):
            terms = local_terms(spans[place]) + terms
            result = add_terms(density, result, coef, operators, first, span, terms)
        elif cut is None:
            result = add_terms(result, result, coef, operators, first, span, terms)
        elif cut == cuts[0]:
            staged = first_piece(result, coef, operators, first, step_modes, cut, arrays)
        elif cut != cuts[-1]:
            staged = next_piece(staged, first, step_modes, cut, arrays)
        else:
            result = last_piece(result, staged, first, step_modes, cut, arrays)
    return result


def solution(mesh):
    placed = (P(("wide", "narrow"), None, None, None), P(), P(), P(), P(), P(), P(), P(), P())
    return jax.shard_map(
        body,
        mesh=mesh,
        in_specs=placed,
        out_specs=P(("wide", "narrow"), None, None, None),
        check_vma=False,
    )
```

```python
import functools

import jax
import jax.numpy as jnp
from jax import lax
from jax.experimental import pallas as pl
from jax.experimental.pallas import tpu as pltpu
from jax.sharding import PartitionSpec as P

VMEM_LIMIT = 56 * 2**20
LAST_VMEM_LIMIT = 24 * 2**20
SMEM = pl.BlockSpec(memory_space=pltpu.SMEM)


def params(flops, moved):
    return dict(
        compiler_params=pltpu.CompilerParams(
            vmem_limit_bytes=VMEM_LIMIT, dimension_semantics=("arbitrary",)
        ),
        cost_estimate=pl.CostEstimate(
            flops=flops, bytes_accessed=moved, transcendentals=0
        ),
    )


def dot(a, b):
    return jnp.dot(a, b, preferred_element_type=jnp.float32)


def round_kernel(groups, low, high, density_ref, _, *refs):
    outs, (source, loads, stores, *rounded) = refs[: len(groups)], refs[len(groups) :]
    pairs = [(index, part) for index in range(low, high) for part in range(2)]
    reads = {
        pair: pltpu.make_async_copy(density_ref.at[pair], source.at[place], loads.at[place])
        for place, pair in enumerate(pairs)
    }
    for pair in pairs:
        reads[pair].start()
    writes = []
    for place, (index, part) in enumerate(pairs):
        reads[index, part].wait()
        kept = rounded[0].at[place]
        kept[...] = source[place].astype(jnp.bfloat16)
        for (first, span, cut), out_ref in zip(groups, outs):
            if not first <= index < first + span or cut and cut[0] != part:
                continue
            rows = pl.ds(cut[1], cut[2]) if cut else pl.ds(0, kept.shape[0])
            target = out_ref.at[index - first, 0 if cut else part]
            writes.append(pltpu.make_async_copy(kept.at[rows], target, stores.at[len(writes)]))
            writes[-1].start()
    for write in writes:
        write.wait()


def round_first_kernel(low, density_ref, out_ref, source, loads):
    span, parts = out_ref.shape[:2]
    pairs = [(index, part) for index in range(span) for part in range(parts)]
    reads = [
        pltpu.make_async_copy(
            density_ref.at[low + index, part], source.at[index, part], loads.at[place]
        )
        for place, (index, part) in enumerate(pairs)
    ]
    for read in reads:
        read.start()
    for read, pair in zip(reads, pairs):
        read.wait()
        out_ref[pair] = source[pair].astype(jnp.bfloat16)


def round_first(density, group):
    n = density.shape[-1]
    low, span, _ = group
    return pl.pallas_call(
        functools.partial(round_first_kernel, low),
        in_specs=[pl.BlockSpec(memory_space=pl.ANY)],
        out_specs=pl.BlockSpec(memory_space=pltpu.VMEM),
        out_shape=pltpu.VMEM((span, 2, n, n), jnp.bfloat16),
        scratch_shapes=[
            pltpu.VMEM((span, 2, n, n), jnp.float32),
            pltpu.SemaphoreType.DMA((2 * span,)),
        ],
        compiler_params=pltpu.CompilerParams(vmem_limit_bytes=VMEM_LIMIT),
        cost_estimate=pl.CostEstimate(
            flops=0, bytes_accessed=n * n * 12 * span, transcendentals=0
        ),
    )(density)


def round_groups(density, groups, after):
    n = density.shape[-1]
    low = min(first for first, _, _ in groups)
    high = max(first + span for first, span, _ in groups)
    parts = 2 * (high - low)
    shapes = [(span, 1, cut[2], n) if cut else (span, 2, n, n) for _, span, cut in groups]
    writes = sum(shape[0] * shape[1] for shape in shapes)
    anywhere = pl.BlockSpec(memory_space=pl.ANY)
    return pl.pallas_call(
        functools.partial(round_kernel, groups, low, high),
        in_specs=[anywhere, anywhere],
        out_specs=[anywhere] * len(groups),
        out_shape=[jax.ShapeDtypeStruct(shape, jnp.bfloat16) for shape in shapes],
        scratch_shapes=[
            pltpu.VMEM((parts, n, n), jnp.float32),
            pltpu.SemaphoreType.DMA((parts,)),
            pltpu.SemaphoreType.DMA((writes,)),
            pltpu.VMEM((parts, n, n), jnp.bfloat16),
        ],
        compiler_params=pltpu.CompilerParams(vmem_limit_bytes=VMEM_LIMIT),
        cost_estimate=pl.CostEstimate(
            flops=0, bytes_accessed=n * n * (4 * parts + 2 * writes), transcendentals=0
        ),
    )(density, after)


def operator_kernel(slot_ref, mask_ref, left_ref, right_ref, ham_ref, lout_ref, rout_ref):
    step = pl.program_id(0)
    last = pl.num_programs(0) - 1
    blocks = mask_ref.shape[2]
    n = left_ref.shape[2]
    size = n // blocks

    @pl.when(step < last)
    def _():
        lane = lax.broadcasted_iota(jnp.int32, (blocks, n), 1)
        row = lax.broadcasted_iota(jnp.int32, (blocks, n), 0)
        spread = jnp.where((lane >= row * size) & (lane < (row + 1) * size), 1.0, 0.0)
        for side, (src, dst) in enumerate(((left_ref, lout_ref), (right_ref, rout_ref))):
            wide = dot(mask_ref[0, side].astype(jnp.float32), spread).astype(jnp.bfloat16)
            for i in range(blocks):
                rows = slice(i * size, (i + 1) * size)
                for part in range(2):
                    dst[0, part, rows, :] = src[0, part, rows, :] * wide[i : i + 1, :]

    @pl.when(step == last)
    def _():
        lout_ref[0, 0] = ham_ref[1]
        lout_ref[0, 1] = -ham_ref[0]
        rout_ref[0, 0] = -ham_ref[1]
        rout_ref[0, 1] = ham_ref[0]


def make_operators(left_operators, right_operators, block_mask, operator_slot, hamiltonian):
    modes, _, n, _ = left_operators.shape
    block = (1, 2, n, n)

    def slot_of(g, slot):
        return (slot[jnp.minimum(g, modes - 1)], 0, 0, 0)

    operator = pl.BlockSpec(block, slot_of)
    out = pl.BlockSpec(block, lambda g, slot: (g, 0, 0, 0))
    shape = jax.ShapeDtypeStruct((modes + 1, 2, n, n), jnp.bfloat16)
    return pl.pallas_call(
        operator_kernel,
        grid_spec=pltpu.PrefetchScalarGridSpec(
            num_scalar_prefetch=1,
            grid=(modes + 1,),
            in_specs=[
                pl.BlockSpec((1,) + block_mask.shape[1:], slot_of),
                operator,
                operator,
                pl.BlockSpec((2, n, n), lambda g, slot: (0, 0, 0)),
            ],
            out_specs=[out, out],
        ),
        out_shape=[shape, shape],
        **params(0, 16 * (modes + 1) * n * n),
    )(operator_slot, block_mask, left_operators, right_operators, hamiltonian)


def term_kernel(first, terms, fresh, coef_ref, base_ref, _, *refs):
    out_ref = refs[-1]
    index = first + pl.program_id(0)
    if fresh:
        rate = -coef_ref[index, coef_ref.shape[1] - 1]
        real, imag = rate * base_ref[0, 0], rate * base_ref[0, 1]
    else:
        real, imag = base_ref[0, 0], base_ref[0, 1]
    for t, mode in enumerate(terms):
        rho, left, right = refs[3 * t : 3 * t + 3]
        coef = coef_ref[index, mode]
        lr, li, rr, ri = left[0, 0], left[0, 1], right[0, 0], right[0, 1]
        a, b = rho[0, 0], rho[0, 1]
        real += coef * (dot(lr, a) - dot(li, b) + dot(a, rr) - dot(b, ri))
        imag += coef * (dot(lr, b) + dot(li, a) + dot(a, ri) + dot(b, rr))
    out_ref[0, 0] = real
    out_ref[0, 1] = imag


def add_terms(base, into, coef, operators, first, span, terms):
    fresh = into is not base
    alias = {1: 0} if not fresh else {2: 0} if into is not None else {}
    into = into if fresh and into is not None else coef
    n = base.shape[-1]
    lefts, rights = operators
    specs, args = [], []
    for mode, array, place in terms:
        specs.append(pl.BlockSpec((1, 2, n, n), lambda g, place=place: (place(g), 0, 0, 0)))
        operator = pl.BlockSpec((1, 2, n, n), lambda g, mode=mode: (mode, 0, 0, 0))
        specs += [operator, operator]
        args += [array, lefts, rights]
    block = pl.BlockSpec((1, 2, n, n), lambda g: (first + g, 0, 0, 0))
    return pl.pallas_call(
        functools.partial(term_kernel, first, [t[0] for t in terms], fresh),
        grid=(span,),
        in_specs=[SMEM, block, pl.BlockSpec(memory_space=pl.ANY)] + specs,
        out_specs=block,
        out_shape=jax.ShapeDtypeStruct(base.shape, jnp.float32),
        input_output_aliases=alias,
        **params(
            16 * n**3 * span * len(terms),
            n * n * span * (16 + 4 * len(terms)) + 8 * n * n * len(terms),
        ),
    )(coef, base, into, *args)


def bands_of(cut, n):
    _, first, size = cut
    bands = [(0, first), (first + size, n), (first, first + size)]
    return [rows for rows in bands if rows[0] < rows[1]]


def add_piece(modes, cut, out, rows, coefs, arrays, left, right, sum_in, sum_out):
    part, first, size = cut
    use = part if out == 0 else 1 - part
    total = sum_in[out, rows[0] : rows[1]]
    for t in range(len(modes)):
        coef = -coefs[t] if out == 0 and part == 1 else coefs[t]
        value = arrays[t][0, 0]
        change = dot(left[t, use, rows[0] : rows[1], first : first + size], value)
        if rows[0] == first:
            change += dot(value, right[t, use])
        total += coef * change
    sum_out[out, rows[0] : rows[1]] = total


def first_piece_kernel(index, modes, cut, coef_ref, base_ref, left_ref, right_ref, *refs):
    count = len(modes)
    arrays, (total, left, right, scale, loads) = refs[:count], refs[count:]
    copies = [pltpu.make_async_copy(base_ref.at[index], total, loads.at[0])]
    for t, mode in enumerate(modes):
        for source, target in ((left_ref, left), (right_ref, right)):
            copies.append(
                pltpu.make_async_copy(source.at[mode], target.at[t], loads.at[len(copies)])
            )
    for copy in copies:
        copy.start()
    coefs = [coef_ref[index, mode] for mode in modes]
    for t in range(count):
        scale[t] = jnp.full(scale.shape[1:], coefs[t])
    for copy in copies:
        copy.wait()
    for out in range(2):
        for rows in bands_of(cut, total.shape[1]):
            add_piece(modes, cut, out, rows, coefs, arrays, left, right, total, total)


def next_piece_kernel(index, modes, cut, total, left, right, scale, *refs):
    arrays, out_ref = refs[:-1], refs[-1]
    coefs = [scale[t, 0:1] for t in range(len(modes))]
    for out in range(2):
        for rows in bands_of(cut, total.shape[1]):
            add_piece(modes, cut, out, rows, coefs, arrays, left, right, total, out_ref)


def last_piece_kernel(index, modes, cut, _, total, left, right, scale, *refs):
    count = len(modes)
    arrays, (out_ref, result, stores) = refs[:count], refs[count:]
    coefs = [scale[t, 0:1] for t in range(count)]
    writes = []
    for out in range(2):
        for rows in bands_of(cut, total.shape[1]):
            add_piece(modes, cut, out, rows, coefs, arrays, left, right, total, result)
            band = pl.ds(rows[0], rows[1] - rows[0])
            writes.append(
                pltpu.make_async_copy(
                    result.at[out, band], out_ref.at[index, out, band], stores.at[len(writes)]
                )
            )
            writes[-1].start()
    for write in writes:
        write.wait()


def in_vmem(array):
    return pltpu.with_memory_space_constraint(array, pltpu.VMEM)


def in_hbm(array):
    return pltpu.with_memory_space_constraint(array, pltpu.HBM)


ANYWHERE = pl.BlockSpec(memory_space=pl.ANY)
WHOLE = pl.BlockSpec(memory_space=pltpu.VMEM)


def piece_call(kernel, index, modes, cut, n, operands, arrays, out_shape, scratch, alias):
    moved = n * n * (16 + 8 * len(modes))
    out_specs = jax.tree.map(
        lambda shape: ANYWHERE if isinstance(shape, jax.ShapeDtypeStruct) else WHOLE, out_shape
    )
    return pl.pallas_call(
        functools.partial(kernel, index, modes, cut),
        in_specs=[spec for _, spec in operands] + [WHOLE] * len(arrays),
        out_specs=out_specs,
        out_shape=out_shape,
        scratch_shapes=scratch,
        input_output_aliases=alias,
        compiler_params=pltpu.CompilerParams(vmem_limit_bytes=LAST_VMEM_LIMIT),
        cost_estimate=pl.CostEstimate(
            flops=8 * n * n * cut[2] * len(modes), bytes_accessed=moved, transcendentals=0
        ),
    )(*[array for array, _ in operands], *[in_vmem(array) for array in arrays])


def first_piece(base, coef, operators, index, modes, cut, arrays):
    n, count = base.shape[-1], len(modes)
    operands = [(coef, SMEM)] + [(in_hbm(array), ANYWHERE) for array in (base, *operators)]
    out_shape = [
        pltpu.VMEM((2, n, n), jnp.float32),
        pltpu.VMEM((count, 2, n, n), jnp.bfloat16),
        pltpu.VMEM((count, 2, n, n), jnp.bfloat16),
        pltpu.VMEM((count, 8, n), jnp.float32),
    ]
    scratch = [pltpu.SemaphoreType.DMA((1 + 2 * count,))]
    return piece_call(
        first_piece_kernel, index, modes, cut, n, operands, arrays, out_shape, scratch, {}
    )


def next_piece(staged, index, modes, cut, arrays):
    n = staged[0].shape[-1]
    operands = [(in_vmem(array), WHOLE) for array in staged]
    out_shape = pltpu.VMEM((2, n, n), jnp.float32)
    total = piece_call(
        next_piece_kernel, index, modes, cut, n, operands, arrays, out_shape, [], {0: 0}
    )
    return [total] + list(staged[1:])


def last_piece(base, staged, index, modes, cut, arrays):
    n = base.shape[-1]
    operands = [(base, ANYWHERE)] + [(in_vmem(array), WHOLE) for array in staged]
    out_shape = jax.ShapeDtypeStruct(base.shape, jnp.float32)
    scratch = [pltpu.VMEM((2, n, n), jnp.float32), pltpu.SemaphoreType.DMA((6,))]
    return piece_call(
        last_piece_kernel, index, modes, cut, n, operands, arrays, out_shape, scratch, {0: 0}
    )


def flip(value, axis, bit):
    pairs = [(source, source ^ (1 << bit)) for source in range(lax.axis_size(axis))]
    return lax.ppermute(value, axis, pairs)


def coefficients(count, modes, flip_sign, damping_rate, lower_weight):
    first = (lax.axis_index("wide") * lax.axis_size("narrow") + lax.axis_index("narrow")) * count
    indices = first + jnp.arange(count, dtype=jnp.int32)
    bits = indices[:, None] >> jnp.arange(modes, dtype=jnp.int32)[None, :] & 1
    parity = 1 - 2 * ((jnp.cumsum(bits, axis=1) - bits) % 2)
    sign = parity * (1 - 2 * flip_sign)[None, :]
    coef = sign.astype(jnp.float32) * jnp.where(bits > 0, lower_weight[None, :], jnp.float32(1.0))
    rates = jnp.sum(bits.astype(jnp.float32) * damping_rate[None, :], axis=1)
    return jnp.concatenate([coef, jnp.ones((count, 1), jnp.float32), rates[:, None]], axis=1)


def body(
    density,
    hamiltonian,
    left_operators,
    right_operators,
    block_mask,
    operator_slot,
    flip_sign,
    damping_rate,
    lower_weight,
):
    count = density.shape[0]
    modes = left_operators.shape[0]
    local_bits = count.bit_length() - 1
    narrow_bits = lax.axis_size("narrow").bit_length() - 1
    last = count - 1

    def axis_of(mode):
        if mode < local_bits + narrow_bits:
            return "narrow", mode - local_bits
        return "wide", mode - local_bits - narrow_bits

    remote = list(range(local_bits, modes))
    slow = remote[-2:][::-1]
    near = [m for m in remote[:-2] if axis_of(m) == ("wide", 0)]
    middle = [m for m in remote[:-2] if m not in near]

    half = count // 2
    spans = [(0, half), (half, half)] if half else [(0, count)]
    pieces = [piece for piece in ((0, half), (half, last - half)) if piece[1]]
    plan = [(near,) + span + (None,) for span in spans]
    plan.append((middle[:1], 0, last or count, None))
    plan += [(slow,) + piece + (None,) for piece in pieces[:1]]
    plan.append((middle[1:], 0, count, None))
    plan += [(slow,) + piece + (None,) for piece in pieces[1:]]
    if last:
        plan.append((middle[:1], last, 1, None))
    n = density.shape[-1]
    cuts = [(0, 0, n), (1, 0, 3 * n // 4), (1, 3 * n // 4, n // 4)]
    plan += [(slow, last, 1, cut) for cut in cuts]

    plan = [step for place, step in enumerate(plan) if step[0] or place < len(spans)]

    groups = list(dict.fromkeys([step[1:] for step in plan]))
    early = [step[1:] for step in plan if step[0] is slow][:1]
    late = [group for group in groups if group not in early]
    if early[0][2] is None:
        rounded = {early[0]: round_first(density, early[0])}
    else:
        rounded = dict(zip(early, round_groups(density, early, damping_rate)))
    rounded.update(zip(late, round_groups(density, late, rounded[early[0]])))

    sent = [[flip(rounded[step[1:]], *axis_of(m)) for m in step[0]] for step in plan]
    coef = coefficients(count, modes, flip_sign, damping_rate, lower_weight)
    operators = make_operators(
        left_operators, right_operators, block_mask, operator_slot, hamiltonian
    )

    def local_terms(span):
        own, other = rounded[span + (None,)], rounded[(half - span[0],) + span[1:] + (None,)]
        terms = [(modes, own, lambda g: g)]
        for mode in range(local_bits):
            step = 1 << mode
            if step < span[1]:
                terms.append((mode, own, lambda g, step=step: g ^ step))
            else:
                terms.append((mode, other, lambda g: g))
        return terms

    result, staged = None, None
    for place, ((step_modes, first, span, cut), arrays) in enumerate(zip(plan, sent)):
        terms = [(m, array, lambda g: g) for m, array in zip(step_modes, arrays)]
        if place < len(spans):
            terms = local_terms(spans[place]) + terms
            result = add_terms(density, result, coef, operators, first, span, terms)
        elif cut is None:
            result = add_terms(result, result, coef, operators, first, span, terms)
        elif cut == cuts[0]:
            staged = first_piece(result, coef, operators, first, step_modes, cut, arrays)
        elif cut != cuts[-1]:
            staged = next_piece(staged, first, step_modes, cut, arrays)
        else:
            result = last_piece(result, staged, first, step_modes, cut, arrays)
    return result


def solution(mesh):
    placed = (P(("wide", "narrow"), None, None, None), P(), P(), P(), P(), P(), P(), P(), P())
    return jax.shard_map(
        body,
        mesh=mesh,
        in_specs=placed,
        out_specs=P(("wide", "narrow"), None, None, None),
        check_vma=False,
    )
```
